32 devices in a mesh: tx: 4 (over x, core), ty: 8 (over z, y).
Axes of the slice: x: 2, y: 2, z: 4, core: 2. Of those that a mesh axis runs over, the one named last changes fastest.
Arguments:
- solution: float32 [4, 512, 2048], P(None, 'tx', 'ty'), may hold values from -6 to 6
- residual: float32 [4, 512, 2048], P(None, 'tx', 'ty')
- direction: float32 [4, 512, 2048], P(None, 'tx', 'ty')
- blocks: bfloat16 [8192, 128, 256], P(('tx', 'ty')), may hold values from -0.375 to 0.375
- bin_owner: int32 [8192, 1], P(('tx', 'ty')), may hold values from 0 to 31; in each aligned block of 256 rows (0 to 255, 256 to 511, ...) at most 12 rows name the same one
- bin_tile: int32 [8192], P(('tx', 'ty')), may hold values from 0 to 127
Outputs:
- next_solution: float32 [4, 512, 2048], P(None, 'tx', 'ty')
- next_residual: float32 [4, 512, 2048], P(None, 'tx', 'ty')
- next_direction: float32 [4, 512, 2048], P(None, 'tx', 'ty')
The draws below stay inside these ranges and needn't reach their ends.
Inputs may be any that keep to these rules, and one draw needn't show every extreme that they name: `bin_owner`: among the bins of one device, at most 12 name the same owner, and on some devices some owner is named by exactly 12 of them.
All inputs are finite; a program needn't handle non-finite values.
Results may differ from the reference program's by a relative error of at most 0.0024.
Values may be sent and summed in bfloat16 or wider, within the bound.
No kernel may reach another device: no remote copies, remote signals or barrier semaphores. Data moves between devices by JAX's collectives and lax.ppermute only.
A program may use at most 128 MiB of HBM per device.

```python
import math
import jax
import jax.numpy as jnp
import numpy as np
from jax import lax

BEACONS = 4
TILE_SIDE = 16
TILE_CELLS = 256
BIN_ROWS = 128
ROWS_DEV = 128
COLS_DEV = 256
BINS_DEV = 256
CAP = 12
TILES_DEV = 128
ROWS = 512
COLS = 2048
BINS = 8192
N_TX = 4
N_TY = 8


def rough_field(key):
    keys = jax.random.split(key, 2)
    rows = jnp.arange(ROWS, dtype=jnp.float32)[:, None] / ROWS
    cols = jnp.arange(COLS, dtype=jnp.float32)[None, :] / COLS
    slope = jnp.exp(math.log(3.0) * (rows + cols)) / 3.0
    beacon = jax.random.uniform(keys[0], (BEACONS, 1, 1), minval=0.5, maxval=2.0)
    scale = slope[None, :, :] * beacon
    noise = jax.random.normal(keys[1], (BEACONS, ROWS, COLS), dtype=jnp.float32)
    return (scale * noise).astype(jnp.float32)


def draw_residual(key, part):
    return rough_field(jax.random.fold_in(key, 11))


def draw_direction(key, part):
    return rough_field(jax.random.fold_in(key, 23))


def set_ends(entries, rng, low, high):
    dims = entries.shape
    index_at = [jax.random.randint(jax.random.fold_in(rng, axis), (), 0, dims[axis]) for axis in range(len(dims))]
    entries = entries.at[tuple(index_at)].set(low)
    longest = dims.index(max(dims))
    index_at[longest] = (index_at[longest] + 1) % dims[longest]
    return entries.at[tuple(index_at)].set(high)


def shard_levels(stream_key, shape, cuts, least, high):
    loudness = 1.0
    for dim, blocks in cuts:
        heights = jax.random.uniform(jax.random.fold_in(jax.random.fold_in(stream_key, 6), dim), (blocks,), jnp.float32, least / len(cuts), high / len(cuts))
        loudness = loudness * jnp.repeat(jnp.exp(heights), shape[dim] // blocks).reshape((-1,) + (1,) * (len(shape) - 1 - dim))
    return loudness


def deal_out(own_key, own, number, rows, count, top, most, skew):
    ranking = jax.random.permutation(own_key, count)
    heavy_load, usual = load_shares(count, rows * top, most, skew, True), load_shares(count, rows * top, most, skew, False)
    places = jnp.arange(count)

    def named(sizes, offset_by):
        used = int((sizes > 0).sum())
        fixed = max(1, used // 4)
        passed = fixed + (places - fixed + offset_by * (used - fixed)) % max(1, count - fixed)
        return jnp.zeros((count,), jnp.int32).at[ranking[jnp.where(places < fixed, places, passed)]].set(jnp.asarray(sizes, jnp.int32))

    sizes = jnp.where(number % 4 == 0, named(heavy_load, number // 4), named(usual, number - number // 4 - 1))
    mixed = jax.random.permutation(jax.random.fold_in(own, 3), count)
    donor, sink = mixed[0:count // 2 * 2:2], mixed[1:count // 2 * 2:2]
    room = jnp.minimum(sizes[donor] - 1, most - sizes[sink]) // 2
    room = jnp.where((donor == ranking[0]) | (sink == ranking[0]) | (sizes[sink] == 0), 0, jnp.maximum(room, 0))
    passed = jax.random.randint(jax.random.fold_in(own, 4), (count // 2,), 0, 1 << 20) % (room + 1)
    sizes = sizes.at[donor].add(-passed).at[sink].add(passed)
    labels = jnp.searchsorted(jnp.cumsum(sizes), jnp.arange(rows * top), side="right").astype(jnp.int32)
    listing = labels.reshape(top, rows).T
    listing = listing[jax.random.permutation(jax.random.fold_in(own, 1), rows)]
    offset_by = jax.random.randint(jax.random.fold_in(own, 2), (rows, 1), 0, top)
    return jnp.take_along_axis(listing, (jnp.arange(top)[None, :] + offset_by) % top, axis=1)


def load_shares(number_of, total, bound, skew, full):
    portions = [(1 << 20) // math.isqrt(standing ** skew) + 1 for standing in range(1, number_of + 1)]
    largest = bound if full else min(bound, max(-(-total // number_of), total * portions[0] // sum(portions)))
    least = 1 if total - largest >= number_of - 1 else 0
    counts, surplus = [largest] + [least] * (number_of - 1), total - largest - least * (number_of - 1)
    while surplus > 0:
        candidates = [i for i in range(1, number_of) if counts[i] < largest] or [i for i in range(1, number_of) if counts[i] < bound]
        mass, left = sum([portions[i] for i in candidates]), surplus
        for i in candidates:
            more = min(bound - counts[i], max(1, left * portions[i] // mass), surplus)
            counts[i] = counts[i] + more
            surplus = surplus - more
    return np.array(counts)


def bell_draw(rng, dims, scale, bound, cuts=(), kind=jnp.bfloat16):
    values = scale * jax.random.normal(rng, dims, jnp.float32)
    if cuts:
        values = values * shard_levels(rng, dims, cuts, -0.22, 0.18)
    return jnp.clip(values, -bound, bound).astype(kind)


def setup_inputs(seed: int = 0) -> dict:
    arg_keys = jax.random.split(jax.random.key(seed), 7)
    solution = bell_draw(arg_keys[0], (BEACONS, ROWS, COLS), 1.0, 6.0, ((1, 4), (2, 8)), jnp.float32)
    residual = draw_residual(jax.random.fold_in(arg_keys[6], 71), 0)
    direction = draw_direction(jax.random.fold_in(arg_keys[6], 71), 0)
    blocks = bell_draw(arg_keys[3], (BINS, BIN_ROWS, TILE_CELLS), TILE_CELLS ** -0.5, 0.375, ((0, 32),))
    bin_owner_keys = jax.random.split(jax.random.fold_in(arg_keys[4], 1), BINS // BINS_DEV)
    bin_owner_turns = jax.random.permutation(jax.random.fold_in(arg_keys[4], 3), BINS // BINS_DEV)
    bin_owner = jax.vmap(lambda own, number: deal_out(jax.random.fold_in(arg_keys[4], 2), own, number, BINS_DEV, N_TX * N_TY, 1, CAP, 2))(bin_owner_keys, bin_owner_turns).reshape((BINS, 1))
    bin_tile = set_ends(jax.random.randint(arg_keys[5], (BINS,), 0, TILES_DEV), jax.random.fold_in(arg_keys[5], 1), 0, TILES_DEV - 1).astype(jnp.int32)
    return dict(solution=solution, residual=residual, direction=direction, blocks=blocks, bin_owner=bin_owner, bin_tile=bin_tile)


smooth_weight = 0.25


def laplace(field):
    padded = jnp.pad(field, ((0, 0), (1, 1), (1, 1)))
    near = padded[:, 2:, 1:-1] + padded[:, :-2, 1:-1] + padded[:, 1:-1, 2:] + padded[:, 1:-1, :-2]
    return 4.0 * field - near


def split_tiles(field):
    across = ROWS_DEV // TILE_SIDE
    down = COLS_DEV // TILE_SIDE
    shaped = field.reshape(BEACONS, N_TX, across, TILE_SIDE, N_TY, down, TILE_SIDE)
    shaped = shaped.transpose(1, 4, 2, 5, 0, 3, 6)
    return shaped.reshape(N_TX * N_TY * across * down, BEACONS, TILE_SIDE * TILE_SIDE)


def join_tiles(tiles):
    across = ROWS_DEV // TILE_SIDE
    down = COLS_DEV // TILE_SIDE
    shaped = tiles.reshape(N_TX, N_TY, across, down, BEACONS, TILE_SIDE, TILE_SIDE)
    shaped = shaped.transpose(4, 0, 2, 5, 1, 3, 6)
    return shaped.reshape(BEACONS, ROWS_DEV * N_TX, COLS_DEV * N_TY)


def reference(solution, residual, direction, blocks, bin_owner, bin_tile):
    devices = N_TX * N_TY
    tiles_dev = (ROWS_DEV // TILE_SIDE) * (COLS_DEV // TILE_SIDE)
    rounded = split_tiles(direction.astype(jnp.bfloat16))
    places = (bin_owner[:, 0] * tiles_dev + bin_tile).astype(jnp.int32)
    weights = blocks.reshape(devices, BINS_DEV, BIN_ROWS, TILE_CELLS)
    places = places.reshape(devices, BINS_DEV)

    def add_device(total, item):
        block, rows_at = item
        picked = rounded[rows_at].astype(jnp.float32)
        wide = block.astype(jnp.float32)
        samples = jnp.einsum("bsc,bkc->bks", wide, picked).astype(jnp.bfloat16)
        adjoint = jnp.einsum("bsc,bks->bkc", wide, samples.astype(jnp.float32))
        return total.at[rows_at].add(adjoint), None

    total, _ = lax.scan(add_device, jnp.zeros(rounded.shape, jnp.float32), (weights, places))
    image = join_tiles(total) + smooth_weight * laplace(direction)
    norm_old = jnp.sum(residual * residual, axis=(1, 2))
    curvature = jnp.sum(direction * image, axis=(1, 2))
    alpha = (norm_old / curvature)[:, None, None]
    next_solution = solution + alpha * direction
    next_residual = residual - alpha * image
    norm_new = jnp.sum(next_residual * next_residual, axis=(1, 2))
    next_direction = next_residual + (norm_new / norm_old)[:, None, None] * direction
    return next_solution, next_residual, next_direction
```

```python
import functools

import jax
import jax.numpy as jnp
from jax import lax
from jax.experimental import pallas as pl
from jax.experimental.pallas import tpu as pltpu
from jax.sharding import PartitionSpec as P

TILE_SIDE = 16
LANES = 128
SUB = 8
smooth_weight = 0.25

AXES = ("tx", "ty")


def whole(memory=pltpu.VMEM):
    return pl.BlockSpec(memory_space=memory)


def params(mib):
    return pltpu.CompilerParams(vmem_limit_bytes=mib << 20)


def swap_chunks(x):
    row = lax.broadcasted_iota(jnp.int32, (SUB, LANES), 0)
    chunk = lax.broadcasted_iota(jnp.int32, (SUB, LANES), 1) // TILE_SIDE
    for s in (1, 2, 4):
        row_bit, chunk_bit = (row & s) != 0, (chunk & s) != 0
        up = pltpu.roll(pltpu.roll(x, SUB - s, 1), TILE_SIDE * s, 2)
        down = pltpu.roll(pltpu.roll(x, s, 1), LANES - TILE_SIDE * s, 2)
        x = jnp.where((row_bit == chunk_bit)[None], x, jnp.where(row_bit[None], down, up))
    return x


def prep_kernel(cap, owner_ref, tile_ref, slot_ref, request_ref):
    devices, bins = request_ref.shape[0], owner_ref.shape[1]
    owner = owner_ref[...]
    member = (lax.broadcasted_iota(jnp.int32, (devices, bins), 0) == owner).astype(jnp.float32)
    earlier = (
        lax.broadcasted_iota(jnp.int32, (bins, bins), 0) < lax.broadcasted_iota(jnp.int32, (bins, bins), 1)
    ).astype(jnp.bfloat16)
    member16 = member.astype(jnp.bfloat16)
    before = jnp.dot(member16, earlier, preferred_element_type=jnp.float32)
    rank = jnp.sum(before * member, axis=0, keepdims=True).astype(jnp.int32)
    slot_ref[...] = owner * cap + rank
    place = lax.broadcasted_iota(jnp.int32, (request_ref.shape[1], bins), 0) == rank
    named = jnp.where(place, tile_ref[...] + 1, 0).astype(jnp.float32).astype(jnp.bfloat16)
    request = lax.dot_general(member16, named, (((1,), (1,)), ((), ())), preferred_element_type=jnp.float32)
    request_ref[...] = request.astype(jnp.int32) - 1


def prep(owner, tile, devices, cap):
    bins = owner.shape[1]
    return pl.pallas_call(
        functools.partial(prep_kernel, cap),
        in_specs=[whole(), whole()],
        out_specs=[whole(), whole()],
        out_shape=[
            jax.ShapeDtypeStruct((1, bins), jnp.int32),
            jax.ShapeDtypeStruct((devices, cap), jnp.int32),
        ],
        compiler_params=params(8),
        name="prep",
    )(owner, tile)


def tiles_kernel(field_ref, out_ref):
    beacons, rows, cols = field_ref.shape
    bands, groups = rows // TILE_SIDE, cols // LANES
    for k in range(beacons):
        for g in range(groups):
            x = field_ref[k, :, g * LANES : (g + 1) * LANES].reshape(bands * 2, SUB, LANES)
            x = swap_chunks(x.astype(jnp.bfloat16).astype(jnp.float32))
            for band in range(bands):
                for h in range(2):
                    at = ((band * groups + g) * 8 + h * beacons + k) * SUB
                    out_ref[at : at + SUB, :] = x[band * 2 + h]


def tiles(field):
    beacons, rows, cols = field.shape
    return pl.pallas_call(
        tiles_kernel,
        in_specs=[whole()],
        out_specs=whole(),
        out_shape=jax.ShapeDtypeStruct((beacons * rows * cols // LANES, LANES), jnp.float32),
        compiler_params=params(8),
        name="tiles",
    )(field)


def gather_kernel(wanted_ref, tiles_ref, out_ref):
    devices, cap = wanted_ref.shape

    def at(d, r):
        t = jnp.maximum(wanted_ref[d, r], 0)
        return tiles_ref[pl.ds((t // SUB) * 64 + t % SUB, SUB, stride=SUB), :]

    def body(d, carry):
        for r in range(0, cap - 1, 2):
            pair = jnp.concatenate([at(d, r), at(d, r + 1)], axis=0)
            out_ref[d, r * SUB : (r + 2) * SUB, :] = pair.astype(jnp.bfloat16)
        if cap % 2:
            pair = jnp.concatenate([at(d, cap - 1), jnp.zeros((SUB, LANES), jnp.float32)], axis=0)
            out_ref[d, (cap - 1) * SUB : (cap + 1) * SUB, :] = pair.astype(jnp.bfloat16)
        return carry

    lax.fori_loop(0, devices, body, 0)


def gather(wanted, own, lines):
    devices = wanted.shape[0]
    return pl.pallas_call(
        gather_kernel,
        in_specs=[whole(pltpu.SMEM), whole()],
        out_specs=whole(),
        out_shape=jax.ShapeDtypeStruct((devices, lines, LANES), jnp.bfloat16),
        compiler_params=params(8),
        name="gather",
    )(wanted, own)


def bins_kernel(chunk, cap, slot_ref, fetched_ref, blocks_ref, out_ref, pick, ret):
    step = pl.program_id(0)
    devices, lines, _ = fetched_ref.shape
    samples, cells = blocks_ref.shape[1:]

    @pl.when(step == 0)
    def _():
        for d in range(devices):
            pick[pl.ds(d * lines, lines), :] = fetched_ref[d].astype(jnp.float32)
            ret[pl.ds(d * lines, lines), :] = jnp.zeros((lines, LANES), jnp.float32)

    low = lax.broadcasted_iota(jnp.int32, (SUB, LANES), 0) < 4
    lane = lax.broadcasted_iota(jnp.int32, (samples, LANES), 1) // 4

    def line(b):
        slot = slot_ref[0, b]
        return pl.multiple_of((slot // cap) * lines + (slot % cap) * SUB if lines != cap * SUB else slot * SUB, SUB)

    for g in range(chunk // 32):
        first = step * chunk + g * 32
        pairs = []
        for p in range(16):
            f0 = pick[pl.ds(line(first + 2 * p), SUB), :]
            f1 = pick[pl.ds(line(first + 2 * p + 1), SUB), :]
            left = jnp.where(low, f0, pltpu.roll(f1, 4, 0))
            right = jnp.where(low, pltpu.roll(f0, 4, 0), f1)
            pairs.append(jnp.concatenate([left, right], axis=1))
        picked = jnp.concatenate(pairs, axis=0).astype(jnp.bfloat16)
        held = jnp.zeros((samples, LANES), jnp.float32)
        for j in range(0, 32, 4):
            m = blocks_ref[pl.ds(g * 32 + j, 4)].reshape(4 * samples, cells)
            s = lax.dot_general(m, picked, (((1,), (1,)), ((), ())), preferred_element_type=jnp.float32)
            for q in range(4):
                held = jnp.where(lane == j + q, s[q * samples : (q + 1) * samples], held)
        held = held.T
        for p in range(16):
            s = held[SUB * p : SUB * p + SUB]
            s = jnp.concatenate([jnp.where(low, s, 0.0), jnp.where(low, 0.0, s)], axis=1).astype(jnp.bfloat16)
            m = blocks_ref[pl.ds(g * 32 + 2 * p, 2)].reshape(2 * samples, cells)
            a = lax.dot_general(s, m, (((1,), (0,)), ((), ())), preferred_element_type=jnp.float32)
            left, right = a[:, :LANES], a[:, LANES:]
            ret[pl.ds(line(first + 2 * p), SUB), :] = jnp.where(low, left, pltpu.roll(right, 4, 0))
            ret[pl.ds(line(first + 2 * p + 1), SUB), :] = jnp.where(low, pltpu.roll(left, 4, 0), right)

    @pl.when(step == pl.num_programs(0) - 1)
    def _():
        for d in range(devices):
            out_ref[d] = ret[pl.ds(d * lines, lines), :].astype(jnp.bfloat16)


def bins(slot, fetched, blocks, cap):
    devices, lines, _ = fetched.shape
    count, samples, cells = blocks.shape
    chunk = 64
    return pl.pallas_call(
        functools.partial(bins_kernel, chunk, cap),
        grid=(count // chunk,),
        in_specs=[
            whole(pltpu.SMEM),
            pl.BlockSpec((devices, lines, LANES), lambda i: (0, 0, 0)),
            pl.BlockSpec((chunk, samples, cells), lambda i: (i, 0, 0)),
        ],
        out_specs=pl.BlockSpec((devices, lines, LANES), lambda i: (0, 0, 0)),
        out_shape=jax.ShapeDtypeStruct((devices, lines, LANES), jnp.bfloat16),
        scratch_shapes=[pltpu.VMEM((devices * lines, LANES), jnp.float32)] * 2,
        compiler_params=params(30),
        name="bins",
    )(slot, fetched, blocks)


def laplace_kernel(field_ref, above_ref, below_ref, sides_ref, out_ref):
    beacons, rows, cols = field_ref.shape
    row = lax.broadcasted_iota(jnp.int32, (rows, cols), 0)
    col = lax.broadcasted_iota(jnp.int32, (rows, cols), 1)
    sides = sides_ref[...].T
    for k in range(beacons):
        x = field_ref[k]
        up = jnp.where(row == 0, above_ref[k : k + 1, :], pltpu.roll(x, 1, 0))
        down = jnp.where(row == rows - 1, below_ref[k : k + 1, :], pltpu.roll(x, rows - 1, 0))
        left = jnp.where(col == 0, sides[:, k : k + 1], pltpu.roll(x, 1, 1))
        right = jnp.where(col == cols - 1, sides[:, beacons + k : beacons + k + 1], pltpu.roll(x, cols - 1, 1))
        out_ref[k] = smooth_weight * (4.0 * x - (down + up + right + left))


def laplace(field, above, below, sides):
    return pl.pallas_call(
        laplace_kernel,
        in_specs=[whole()] * 4,
        out_specs=whole(),
        out_shape=jax.ShapeDtypeStruct(field.shape, jnp.float32),
        compiler_params=params(8),
        name="laplace",
    )(field, above, below, sides)


def image_kernel(wanted_ref, arrived_ref, smooth_ref, direction_ref, residual_ref, image_ref, stats_ref, even, odd):
    devices, cap = wanted_ref.shape
    beacons, rows, cols = direction_ref.shape
    bands, groups = rows // TILE_SIDE, cols // LANES
    even[...] = jnp.zeros_like(even)
    odd[...] = jnp.zeros_like(odd)

    def body(d, carry):
        for r in range(0, cap, 2):
            pair = arrived_ref[d, r * SUB : (r + 2) * SUB, :].astype(jnp.float32)
            at = pl.ds(pl.multiple_of(jnp.maximum(wanted_ref[d, r], 0) * SUB, SUB), SUB)
            even[at, :] += pair[:SUB]
            if r + 1 < cap:
                at = pl.ds(pl.multiple_of(jnp.maximum(wanted_ref[d, r + 1], 0) * SUB, SUB), SUB)
                odd[at, :] += pair[SUB:]
        return carry

    lax.fori_loop(0, devices, body, 0)
    lane = lax.broadcasted_iota(jnp.int32, (1, LANES), 1)
    stats = jnp.zeros((1, LANES), jnp.float32)
    for k in range(beacons):
        largest = jnp.zeros((SUB, LANES), jnp.float32)
        for g in range(groups):
            x = []
            for band in range(bands):
                for h in range(2):
                    at = pl.ds((band * groups + g) * 64 + h * beacons + k, SUB, stride=SUB)
                    x.append(even[at, :] + odd[at, :])
            x = swap_chunks(jnp.stack(x)).reshape(rows, LANES)
            x = x + smooth_ref[k, :, g * LANES : (g + 1) * LANES]
            image_ref[k, :, g * LANES : (g + 1) * LANES] = x
            largest = jnp.maximum(largest, jnp.max(jnp.abs(x).reshape(bands * 2, SUB, LANES), axis=0))
        largest = jnp.maximum(jnp.max(largest, axis=(0, 1), keepdims=True), 1e-30)
        x, d, r = image_ref[k], direction_ref[k], residual_ref[k]
        scaled = x * (1.0 / largest)
        for q, term in enumerate((r * r, d * x, r * scaled, scaled * scaled)):
            stats = jnp.where(lane == q * beacons + k, jnp.sum(term, axis=(0, 1), keepdims=True), stats)
        stats = jnp.where(lane == 4 * beacons + k, largest, stats)
    stats_ref[...] = jnp.broadcast_to(stats, stats_ref.shape)


def image_of(wanted, arrived, smooth, direction, residual):
    beacons, rows, cols = direction.shape
    return pl.pallas_call(
        image_kernel,
        in_specs=[whole(pltpu.SMEM)] + [whole()] * 4,
        out_specs=[whole(), whole()],
        out_shape=[
            jax.ShapeDtypeStruct(direction.shape, jnp.float32),
            jax.ShapeDtypeStruct((wanted.shape[0], LANES), jnp.float32),
        ],
        scratch_shapes=[pltpu.VMEM((beacons * rows * cols // LANES, LANES), jnp.float32)] * 2,
        compiler_params=params(16),
        name="image",
    )(wanted, arrived, smooth, direction, residual)


def update_kernel(beacons, stats_ref, solution_ref, residual_ref, direction_ref, image_ref, sol_ref, res_ref, dir_ref):
    k = pl.program_id(0)
    stats = stats_ref[...]
    lane = lax.broadcasted_iota(jnp.int32, stats.shape, 1)

    def column(q):
        return jnp.sum(jnp.where(lane == q * beacons + k, stats, 0.0), axis=1, keepdims=True)

    rr, di, ri, ii, unit = (column(q) for q in range(5))
    norm_old = jnp.sum(rr, axis=0, keepdims=True)
    alpha = norm_old / jnp.sum(di, axis=0, keepdims=True)
    size = alpha * unit
    norm_new = norm_old + jnp.sum(size * (size * ii - 2.0 * ri), axis=0, keepdims=True)
    beta = norm_new / norm_old
    d = direction_ref[...][0]
    res = residual_ref[...][0] - alpha * image_ref[...][0]
    sol_ref[...] = (solution_ref[...][0] + alpha * d)[None]
    res_ref[...] = res[None]
    dir_ref[...] = (res + beta * d)[None]


def update(stats, solution, residual, direction, image):
    beacons, rows, cols = direction.shape
    block = pl.BlockSpec((1, rows, cols), lambda k: (k, 0, 0))
    return pl.pallas_call(
        functools.partial(update_kernel, beacons),
        grid=(beacons,),
        in_specs=[pl.BlockSpec(stats.shape, lambda k: (0, 0))] + [block] * 4,
        out_specs=[block] * 3,
        out_shape=[jax.ShapeDtypeStruct(direction.shape, jnp.float32)] * 3,
        compiler_params=params(8),
        name="update",
    )(stats, solution, residual, direction, image)


def exchange(x):
    return lax.all_to_all(x, AXES, split_axis=0, concat_axis=0, tiled=True)


def shift(x, axis, step):
    size = lax.axis_size(axis)
    return lax.ppermute(x, axis, [(i, i + step) for i in range(size) if 0 <= i + step < size])


def per_device(solution, residual, direction, blocks, bin_owner, bin_tile):
    devices = lax.axis_size("tx") * lax.axis_size("ty")
    count = blocks.shape[0]
    cap = max(2, 3 * count // (2 * devices))
    lines = -(-cap // 2) * 2 * SUB

    slot, request = prep(bin_owner.reshape(1, count), bin_tile.reshape(1, count), devices, cap)
    wanted = exchange(request)
    own = tiles(direction)
    edges = direction.astype(jnp.bfloat16)
    above = shift(edges[:, -1, :], "tx", 1).astype(jnp.float32)
    below = shift(edges[:, 0, :], "tx", -1).astype(jnp.float32)
    left = shift(edges[:, :, -1], "ty", 1).astype(jnp.float32)
    right = shift(edges[:, :, 0], "ty", -1).astype(jnp.float32)
    smooth = laplace(direction, above, below, jnp.concatenate([left, right], axis=0))
    fetched = exchange(gather(wanted, own, lines))
    arrived = exchange(bins(slot, fetched, blocks, cap))
    image, stats = image_of(wanted, arrived, smooth, direction, residual)
    return update(exchange(stats), solution, residual, direction, image)


def solution(mesh):
    placed = (
        P(None, "tx", "ty"),
        P(None, "tx", "ty"),
        P(None, "tx", "ty"),
        P(AXES, None, None),
        P(AXES, None),
        P(AXES),
    )
    return jax.shard_map(
        per_device,
        mesh=mesh,
        in_specs=placed,
        out_specs=(P(None, "tx", "ty"),) * 3,
        check_vma=False,
    )
```

```python
import functools

import jax
import jax.numpy as jnp
from jax import lax
from jax.experimental import pallas as pl
from jax.experimental.pallas import tpu as pltpu
from jax.sharding import PartitionSpec as P

TILE_SIDE = 16
LANES = 128
SUB = 8
smooth_weight = 0.25

AXES = ("tx", "ty")


def whole(memory=pltpu.VMEM):
    return pl.BlockSpec(memory_space=memory)


def params(mib):
    return pltpu.CompilerParams(vmem_limit_bytes=mib << 20)


def swap_chunks(x):
    row = lax.broadcasted_iota(jnp.int32, (SUB, LANES), 0)
    chunk = lax.broadcasted_iota(jnp.int32, (SUB, LANES), 1) // TILE_SIDE
    for s in (1, 2, 4):
        row_bit, chunk_bit = (row & s) != 0, (chunk & s) != 0
        other = pltpu.roll(pltpu.roll(x, s, 1), LANES - TILE_SIDE * s, 2)
        if s < 4:
            up = pltpu.roll(pltpu.roll(x, SUB - s, 1), TILE_SIDE * s, 2)
            other = jnp.where(row_bit[None], other, up)
        x = jnp.where((row_bit == chunk_bit)[None], x, other)
    return x


def prep_kernel(cap, owner_ref, tile_ref, slot_ref, request_ref):
    devices, bins = request_ref.shape[0], owner_ref.shape[1]
    owner = owner_ref[...]
    member = (lax.broadcasted_iota(jnp.int32, (devices, bins), 0) == owner).astype(jnp.float32)
    earlier = (
        lax.broadcasted_iota(jnp.int32, (bins, bins), 0) < lax.broadcasted_iota(jnp.int32, (bins, bins), 1)
    ).astype(jnp.bfloat16)
    member16 = member.astype(jnp.bfloat16)
    before = jnp.dot(member16, earlier, preferred_element_type=jnp.float32)
    rank = jnp.sum(before * member, axis=0, keepdims=True).astype(jnp.int32)
    slot_ref[...] = owner * cap + rank
    place = lax.broadcasted_iota(jnp.int32, (request_ref.shape[1], bins), 0) == rank
    named = jnp.where(place, tile_ref[...] + 1, 0).astype(jnp.float32).astype(jnp.bfloat16)
    request = lax.dot_general(member16, named, (((1,), (1,)), ((), ())), preferred_element_type=jnp.float32)
    request_ref[...] = request.astype(jnp.int32) - 1


def prep(owner, tile, devices, cap):
    bins = owner.shape[1]
    return pl.pallas_call(
        functools.partial(prep_kernel, cap),
        in_specs=[whole(), whole()],
        out_specs=[whole(), whole()],
        out_shape=[
            jax.ShapeDtypeStruct((1, bins), jnp.int32),
            jax.ShapeDtypeStruct((devices, cap), jnp.int32),
        ],
        compiler_params=params(60),
        name="prep",
    )(owner, tile)


def tiles_kernel(field_ref, out_ref, top_ref, bottom_ref, sides_ref):
    beacons, rows, cols = field_ref.shape
    bands, groups = rows // TILE_SIDE, cols // LANES
    for k in range(beacons):
        for g in range(groups):
            x = field_ref[k, :, g * LANES : (g + 1) * LANES].reshape(bands * 2, SUB, LANES)
            x = swap_chunks(x.astype(jnp.bfloat16).astype(jnp.float32))
            for band in range(bands):
                for h in range(2):
                    at = (band * groups + g) * SUB * SUB + h * beacons + k
                    out_ref[pl.ds(at, SUB, stride=SUB), :] = x[band * 2 + h]
    top_ref[...] = field_ref[:, 0, :].astype(jnp.bfloat16)
    bottom_ref[...] = field_ref[:, rows - 1, :].astype(jnp.bfloat16)
    lane = lax.broadcasted_iota(jnp.int32, (rows, LANES), 1)
    ends = jnp.zeros((rows, LANES), jnp.float32)
    for k in range(beacons):
        ends = jnp.where(lane == k, field_ref[k, :, cols - 1 :], ends)
        ends = jnp.where(lane == beacons + k, field_ref[k, :, :1], ends)
    sides_ref[...] = ends.T[: 2 * beacons].astype(jnp.bfloat16)


def tiles(field):
    beacons, rows, cols = field.shape
    return pl.pallas_call(
        tiles_kernel,
        in_specs=[whole()],
        out_specs=[whole()] * 4,
        out_shape=[
            jax.ShapeDtypeStruct((beacons * rows * cols // LANES, LANES), jnp.float32),
            jax.ShapeDtypeStruct((beacons, cols), jnp.bfloat16),
            jax.ShapeDtypeStruct((beacons, cols), jnp.bfloat16),
            jax.ShapeDtypeStruct((2 * beacons, rows), jnp.bfloat16),
        ],
        compiler_params=params(8),
        name="tiles",
    )(field)


def gather_kernel(wanted_ref, tiles_ref, out_ref):
    devices, cap = wanted_ref.shape

    def at(d, r):
        return tiles_ref[pl.ds(pl.multiple_of(jnp.maximum(wanted_ref[d, r], 0) * SUB, SUB), SUB), :]

    def body(d, carry):
        for r in range(0, cap - 1, 2):
            pair = jnp.concatenate([at(d, r), at(d, r + 1)], axis=0)
            out_ref[d, r * SUB : (r + 2) * SUB, :] = pair.astype(jnp.bfloat16)
        if cap % 2:
            pair = jnp.concatenate([at(d, cap - 1), jnp.zeros((SUB, LANES), jnp.float32)], axis=0)
            out_ref[d, (cap - 1) * SUB : (cap + 1) * SUB, :] = pair.astype(jnp.bfloat16)
        return carry

    lax.fori_loop(0, devices, body, 0, unroll=4)


def gather(wanted, own, lines):
    devices = wanted.shape[0]
    return pl.pallas_call(
        gather_kernel,
        in_specs=[whole(pltpu.SMEM), whole()],
        out_specs=whole(),
        out_shape=jax.ShapeDtypeStruct((devices, lines, LANES), jnp.bfloat16),
        compiler_params=params(8),
        name="gather",
    )(wanted, own)


def bins_kernel(group, cap, slot_ref, fetched_ref, blocks_ref, out_ref, held, pick, ret, sems):
    devices, lines, _ = fetched_ref.shape
    count, samples, cells = blocks_ref.shape

    def fetch(i):
        part = pl.ds(i * group, group)
        return pltpu.make_async_copy(blocks_ref.at[part], held.at[part], sems.at[i])

    for i in range(count // group):
        fetch(i).start()
    for d in range(devices):
        pick[pl.ds(d * lines, lines), :] = fetched_ref[d].astype(jnp.float32)
        ret[pl.ds(d * lines, lines), :] = jnp.zeros((lines, LANES), jnp.float32)
    low = lax.broadcasted_iota(jnp.int32, (SUB, LANES), 0) < 4

    def line(b):
        slot = slot_ref[0, b]
        at = slot * SUB if lines == cap * SUB else (slot // cap) * lines + (slot % cap) * SUB
        return pl.multiple_of(at, SUB)

    def body(i, carry):
        fetch(i).wait()
        first = i * group
        sampled = []
        for p in range(group // 2):
            f0 = pick[pl.ds(line(first + 2 * p), SUB), :]
            f1 = pick[pl.ds(line(first + 2 * p + 1), SUB), :]
            left = jnp.where(low, f0, pltpu.roll(f1, 4, 0))
            right = jnp.where(low, pltpu.roll(f0, 4, 0), f1)
            x = jnp.concatenate([left, right], axis=1).astype(jnp.bfloat16)
            m = held[pl.ds(first + 2 * p, 2)].reshape(2 * samples, cells)
            s = lax.dot_general(x, m, (((1,), (1,)), ((), ())), preferred_element_type=jnp.float32)
            s = jnp.concatenate([jnp.where(low, s[:, :samples], 0.0), jnp.where(low, 0.0, s[:, samples:])], axis=1)
            sampled.append(s.astype(jnp.bfloat16))
        for p in range(group // 2):
            m = held[pl.ds(first + 2 * p, 2)].reshape(2 * samples, cells)
            a = jnp.dot(sampled[p], m, preferred_element_type=jnp.float32)
            left, right = a[:, :LANES], a[:, LANES:]
            ret[pl.ds(line(first + 2 * p), SUB), :] = jnp.where(low, left, pltpu.roll(right, 4, 0))
            ret[pl.ds(line(first + 2 * p + 1), SUB), :] = jnp.where(low, pltpu.roll(left, 4, 0), right)
        return carry

    lax.fori_loop(0, count // group, body, 0)
    for d in range(devices):
        out_ref[d] = ret[pl.ds(d * lines, lines), :].astype(jnp.bfloat16)


def bins(slot, fetched, blocks, cap):
    devices, lines, _ = fetched.shape
    group = 32
    return pl.pallas_call(
        functools.partial(bins_kernel, group, cap),
        in_specs=[whole(pltpu.SMEM), whole(), whole(pl.ANY)],
        out_specs=whole(),
        out_shape=jax.ShapeDtypeStruct((devices, lines, LANES), jnp.bfloat16),
        scratch_shapes=[
            pltpu.VMEM(blocks.shape, jnp.bfloat16),
            pltpu.VMEM((devices * lines, LANES), jnp.float32),
            pltpu.VMEM((devices * lines, LANES), jnp.float32),
            pltpu.SemaphoreType.DMA((blocks.shape[0] // group,)),
        ],
        compiler_params=params(50),
        name="bins",
    )(slot, fetched, blocks)


def laplace_kernel(field_ref, above_ref, below_ref, left_ref, right_ref, out_ref):
    beacons, rows, cols = field_ref.shape
    row = lax.broadcasted_iota(jnp.int32, (rows, cols), 0)
    col = lax.broadcasted_iota(jnp.int32, (rows, cols), 1)
    above, below = above_ref[...].astype(jnp.float32), below_ref[...].astype(jnp.float32)
    sides = jnp.concatenate([left_ref[...].astype(jnp.float32), right_ref[...].astype(jnp.float32)], axis=0).T
    for k in range(beacons):
        x = field_ref[k]
        up = jnp.where(row == 0, above[k : k + 1, :], pltpu.roll(x, 1, 0))
        down = jnp.where(row == rows - 1, below[k : k + 1, :], pltpu.roll(x, rows - 1, 0))
        left = jnp.where(col == 0, sides[:, k : k + 1], pltpu.roll(x, 1, 1))
        right = jnp.where(col == cols - 1, sides[:, beacons + k : beacons + k + 1], pltpu.roll(x, cols - 1, 1))
        out_ref[k] = smooth_weight * (4.0 * x - (down + up + right + left))


def laplace(field, above, below, left, right):
    return pl.pallas_call(
        laplace_kernel,
        in_specs=[whole()] * 5,
        out_specs=whole(),
        out_shape=jax.ShapeDtypeStruct(field.shape, jnp.float32),
        compiler_params=params(8),
        name="laplace",
    )(field, above, below, left, right)


def image_kernel(wanted_ref, arrived_ref, smooth_ref, direction_ref, residual_ref, image_ref, stats_ref, *sums):
    devices, cap = wanted_ref.shape
    beacons, rows, cols = direction_ref.shape
    bands, groups = rows // TILE_SIDE, cols // LANES
    for total in sums:
        total[...] = jnp.zeros_like(total)

    def body(d, carry):
        for r in range(0, cap, 2):
            pair = arrived_ref[d, r * SUB : (r + 2) * SUB, :].astype(jnp.float32)
            for q in range(min(2, cap - r)):
                at = pl.ds(pl.multiple_of(jnp.maximum(wanted_ref[d, r + q], 0) * SUB, SUB), SUB)
                sums[(r + q) % len(sums)][at, :] += pair[q * SUB : (q + 1) * SUB]
        return carry

    lax.fori_loop(0, devices, body, 0, unroll=2)
    lines = []
    units = []
    for k in range(beacons):
        unit = jnp.zeros((SUB, LANES), jnp.float32)
        for g in range(groups):
            x = []
            for band in range(bands):
                for h in range(2):
                    at = pl.ds((band * groups + g) * SUB * SUB + h * beacons + k, SUB, stride=SUB)
                    x.append(sum(total[at, :] for total in sums))
            x = swap_chunks(jnp.stack(x)).reshape(rows, LANES)
            x = x + smooth_ref[k, :, g * LANES : (g + 1) * LANES]
            image_ref[k, :, g * LANES : (g + 1) * LANES] = x
            unit = jnp.maximum(unit, jnp.max(jnp.abs(x).reshape(bands * 2, SUB, LANES), axis=0))
        unit = jnp.maximum(unit, 1e-30)
        inverse = 1.0 / unit
        terms = [jnp.zeros((SUB, LANES), jnp.float32)] * 4
        for i in range(rows // SUB):
            for g in range(groups):
                at = (k, slice(i * SUB, (i + 1) * SUB), slice(g * LANES, (g + 1) * LANES))
                x, d, r = image_ref[at], direction_ref[at], residual_ref[at]
                scaled = x * inverse
                terms = [t + v for t, v in zip(terms, (r * r, d * x, r * scaled, scaled * scaled))]
        lines.append(terms)
        units.append(unit)
    largest = [jnp.max(unit, axis=(0, 1), keepdims=True) for unit in units]
    rows_of = []
    for q in range(4):
        for k in range(beacons):
            t = lines[k][q]
            if q >= 2:
                share = units[k] * (1.0 / largest[k])
                t = t * share if q == 2 else t * share * share
            rows_of.append(jnp.sum(t, axis=0, keepdims=True))
    for k in range(beacons):
        first = lax.broadcasted_iota(jnp.int32, (1, LANES), 1) == 0
        rows_of.append(jnp.where(first, largest[k], 0.0))
    rows_of.append(jnp.zeros((LANES - len(rows_of), LANES), jnp.float32))
    stats = jnp.sum(jnp.concatenate(rows_of, axis=0).T, axis=0, keepdims=True)
    stats_ref[...] = jnp.broadcast_to(stats, stats_ref.shape)


def image_of(wanted, arrived, smooth, direction, residual):
    beacons, rows, cols = direction.shape
    return pl.pallas_call(
        image_kernel,
        in_specs=[whole(pltpu.SMEM)] + [whole()] * 4,
        out_specs=[whole(), whole()],
        out_shape=[
            jax.ShapeDtypeStruct(direction.shape, jnp.float32),
            jax.ShapeDtypeStruct((wanted.shape[0], LANES), jnp.float32),
        ],
        scratch_shapes=[pltpu.VMEM((beacons * rows * cols // LANES, LANES), jnp.float32)] * 4,
        compiler_params=params(16),
        name="image",
    )(wanted, arrived, smooth, direction, residual)


def update_kernel(
    stats_ref, solution_ref, residual_ref, direction_ref, image_ref, sol_ref, res_ref, dir_ref, sol, res, dire, sems
):
    beacons = direction_ref.shape[0]
    stats = stats_ref[...]

    def column(x, q):
        return pltpu.roll(x, LANES - q * beacons, 1) if q else x

    total = jnp.sum(stats, axis=0, keepdims=True)
    total = jnp.broadcast_to(total, (SUB, LANES))
    alpha = total / column(total, 1)
    size = alpha[:1] * column(stats, 4)
    moved = jnp.sum(size * (size * column(stats, 3) - 2.0 * column(stats, 2)), axis=0, keepdims=True)
    beta = (total + moved) / total
    copies = []
    for k in range(beacons):
        a, b = alpha[:1, k : k + 1], beta[:1, k : k + 1]
        d = direction_ref[k]
        r = residual_ref[k] - a * image_ref[k]
        sol[k] = solution_ref[k] + a * d
        res[k] = r
        dire[k] = r + b * d
        for q, (held, out) in enumerate(((sol, sol_ref), (res, res_ref), (dire, dir_ref))):
            copies.append(pltpu.make_async_copy(held.at[k], out.at[k], sems.at[q, k]))
            copies[-1].start()
    for copy in copies:
        copy.wait()


def update(stats, solution, residual, direction, image):
    return pl.pallas_call(
        update_kernel,
        in_specs=[whole()] * 5,
        out_specs=[whole(pl.ANY)] * 3,
        out_shape=[jax.ShapeDtypeStruct(direction.shape, jnp.float32)] * 3,
        scratch_shapes=[pltpu.VMEM(direction.shape, jnp.float32)] * 3
        + [pltpu.SemaphoreType.DMA((3, direction.shape[0]))],
        compiler_params=params(16),
        name="update",
    )(stats, solution, residual, direction, image)


def exchange(x):
    return lax.all_to_all(x, AXES, split_axis=0, concat_axis=0, tiled=True)


def shift(x, axis, step):
    size = lax.axis_size(axis)
    return lax.ppermute(x, axis, [(i, i + step) for i in range(size) if 0 <= i + step < size])


def per_device(solution, residual, direction, blocks, bin_owner, bin_tile):
    devices = lax.axis_size("tx") * lax.axis_size("ty")
    count = blocks.shape[0]
    cap = max(2, 3 * count // (2 * devices))
    lines = -(-cap // 2) * 2 * SUB

    slot, request = prep(bin_owner.reshape(1, count), bin_tile.reshape(1, count), devices, cap)
    wanted = exchange(request)
    own, top, bottom, sides = tiles(direction)
    above, below = shift(bottom, "tx", 1), shift(top, "tx", -1)
    beacons = direction.shape[0]
    left, right = shift(sides[:beacons], "ty", 1), shift(sides[beacons:], "ty", -1)
    smooth = laplace(direction, above, below, left, right)
    fetched = exchange(gather(wanted, own, lines))
    arrived = exchange(bins(slot, fetched, blocks, cap))
    image, stats = image_of(wanted, arrived, smooth, direction, residual)
    return update(exchange(stats), solution, residual, direction, image)


def solution(mesh):
    placed = (
        P(None, "tx", "ty"),
        P(None, "tx", "ty"),
        P(None, "tx", "ty"),
        P(AXES, None, None),
        P(AXES, None),
        P(AXES),
    )
    return jax.shard_map(
        per_device,
        mesh=mesh,
        in_specs=placed,
        out_specs=(P(None, "tx", "ty"),) * 3,
        check_vma=False,
    )
```

```python
import functools

import jax
import jax.numpy as jnp
from jax import lax
from jax.experimental import pallas as pl
from jax.experimental.pallas import tpu as pltpu
from jax.sharding import PartitionSpec as P

TILE_SIDE = 16
LANES = 128
SUB = 8
smooth_weight = 0.25

AXES = ("tx", "ty")


def whole(memory=pltpu.VMEM):
    return pl.BlockSpec(memory_space=memory)


def params(mib):
    return pltpu.CompilerParams(vmem_limit_bytes=mib << 20)


def swap_chunks(x):
    row = lax.broadcasted_iota(jnp.int32, (SUB, LANES), 0)
    chunk = SUB - 1 - lax.broadcasted_iota(jnp.int32, (SUB, LANES), 1) // TILE_SIDE
    x = pltpu.roll(x, 0, 2, stride=TILE_SIDE, stride_axis=1)
    for s in (1, 2, 4):
        x = jnp.where(((chunk & s) != 0)[None], pltpu.roll(x, s, 1), x)
    x = pltpu.roll(x, TILE_SIDE, 2, stride=TILE_SIDE, stride_axis=1)
    x = pltpu.roll(x, 4, 1)
    for s in (1, 2):
        x = jnp.where(((row & s) != 0)[None], pltpu.roll(x, s, 1), pltpu.roll(x, SUB - s, 1))
    return x


def prep_kernel(step, owner_hbm, tile_hbm, line_ref, request_ref, owner_ref, tile_ref, sems):
    devices, bins = request_ref.shape[0], owner_ref.shape[1]
    copies = [
        pltpu.make_async_copy(a, b, sems.at[i])
        for i, (a, b) in enumerate(((owner_hbm, owner_ref), (tile_hbm, tile_ref)))
    ]
    for copy in copies:
        copy.start()
    earlier = (
        lax.broadcasted_iota(jnp.int32, (bins, bins), 0) < lax.broadcasted_iota(jnp.int32, (bins, bins), 1)
    ).astype(jnp.bfloat16)
    copies[0].wait()
    owner = owner_ref[...]
    member = (lax.broadcasted_iota(jnp.int32, (devices, bins), 0) == owner).astype(jnp.float32)
    member16 = member.astype(jnp.bfloat16)
    before = jnp.dot(member16, earlier, preferred_element_type=jnp.float32)
    rank = jnp.sum(before * member, axis=0, keepdims=True).astype(jnp.int32)
    line_ref[...] = owner * step + rank * SUB
    place = lax.broadcasted_iota(jnp.int32, (request_ref.shape[1], bins), 0) == rank
    copies[1].wait()
    named = jnp.where(place, tile_ref[...], 0).astype(jnp.float32).astype(jnp.bfloat16)
    request = lax.dot_general(member16, named, (((1,), (1,)), ((), ())), preferred_element_type=jnp.float32)
    request_ref[...] = request.astype(jnp.int32) * SUB


def prep(owner, tile, devices, cap, lines):
    bins = owner.shape[1]
    return pl.pallas_call(
        functools.partial(prep_kernel, lines),
        in_specs=[whole(pl.ANY)] * 2,
        out_specs=[whole()] * 2,
        out_shape=[
            jax.ShapeDtypeStruct((1, bins), jnp.int32),
            jax.ShapeDtypeStruct((devices, cap), jnp.int32),
        ],
        scratch_shapes=[pltpu.VMEM((1, bins), jnp.int32)] * 2 + [pltpu.SemaphoreType.DMA((2,))],
        compiler_params=params(60),
        name="prep",
    )(owner, tile)


def tiles_kernel(field_ref, out_ref, top_ref, bottom_ref, sides_ref):
    beacons, rows, cols = field_ref.shape
    bands, groups = rows // TILE_SIDE, cols // LANES
    for k in range(beacons):
        for g in range(groups):
            x = field_ref[k, :, g * LANES : (g + 1) * LANES].reshape(bands * 2, SUB, LANES)
            x = swap_chunks(x.astype(jnp.bfloat16).astype(jnp.float32))
            for band in range(bands):
                for h in range(2):
                    at = (band * groups + g) * SUB * SUB + h * beacons + k
                    out_ref[pl.ds(at, SUB, stride=SUB), :] = x[band * 2 + h]
    top_ref[...] = field_ref[:, 0, :].astype(jnp.bfloat16)
    bottom_ref[...] = field_ref[:, rows - 1, :].astype(jnp.bfloat16)
    lane = lax.broadcasted_iota(jnp.int32, (rows, LANES), 1)
    ends = jnp.zeros((rows, LANES), jnp.float32)
    for k in range(beacons):
        ends = jnp.where(lane == k, field_ref[k, :, cols - 1 :], ends)
        ends = jnp.where(lane == beacons + k, field_ref[k, :, :1], ends)
    sides_ref[...] = ends.T[: 2 * beacons].astype(jnp.bfloat16)


def tiles(field):
    beacons, rows, cols = field.shape
    return pl.pallas_call(
        tiles_kernel,
        in_specs=[whole()],
        out_specs=[whole()] * 4,
        out_shape=[
            jax.ShapeDtypeStruct((beacons * rows * cols // LANES, LANES), jnp.float32),
            jax.ShapeDtypeStruct((beacons, cols), jnp.bfloat16),
            jax.ShapeDtypeStruct((beacons, cols), jnp.bfloat16),
            jax.ShapeDtypeStruct((2 * beacons, rows), jnp.bfloat16),
        ],
        compiler_params=params(8),
        name="tiles",
    )(field)


def gather_kernel(wanted_ref, tiles_ref, out_ref):
    devices, cap = wanted_ref.shape

    def at(d, r):
        return tiles_ref[pl.ds(pl.multiple_of(wanted_ref[d, r], SUB), SUB), :]

    def body(d, carry):
        for r in range(0, cap - 1, 2):
            pair = jnp.concatenate([at(d, r), at(d, r + 1)], axis=0)
            out_ref[d, r * SUB : (r + 2) * SUB, :] = pair.astype(jnp.bfloat16)
        if cap % 2:
            pair = jnp.concatenate([at(d, cap - 1), jnp.zeros((SUB, LANES), jnp.float32)], axis=0)
            out_ref[d, (cap - 1) * SUB : (cap + 1) * SUB, :] = pair.astype(jnp.bfloat16)
        return carry

    lax.fori_loop(0, devices, body, 0, unroll=4)


def gather(wanted, own, lines):
    devices = wanted.shape[0]
    return pl.pallas_call(
        gather_kernel,
        in_specs=[whole(pltpu.SMEM), whole()],
        out_specs=whole(),
        out_shape=jax.ShapeDtypeStruct((devices, lines, LANES), jnp.bfloat16),
        compiler_params=params(8),
        name="gather",
    )(wanted, own)


def bins_kernel(
    group, line_ref, fetched_ref, blocks_ref, out_ref, held_ref, turn_a, turn_b, samp_a, samp_b, pick, ret, sems
):
    devices, lines, _ = fetched_ref.shape
    count, samples, cells = blocks_ref.shape
    groups, pairs = count // group, group // 2

    def fetch(i):
        part = pl.ds(i * group, group)
        return pltpu.make_async_copy(blocks_ref.at[part], held_ref.at[part], sems.at[i])

    for i in range(groups):
        fetch(i).start()
    for d in range(devices):
        pick[pl.ds(d * lines, lines), :] = fetched_ref[d].astype(jnp.float32)
        ret[pl.ds(d * lines, lines), :] = jnp.zeros((lines, LANES), jnp.float32)
    samp_b[...] = jnp.zeros_like(samp_b)
    low = lax.broadcasted_iota(jnp.int32, (SUB, LANES), 0) < 4

    def weights(g, p):
        return held_ref[pl.ds(g * group + 2 * p, 2)].reshape(2 * samples, cells)

    def turn(g, to):
        for p in range(pairs):
            to[p] = weights(g, p).T

    def line(b):
        return pl.ds(pl.multiple_of(line_ref[0, b], SUB), SUB)

    def sample(g, turned, to):
        for p in range(pairs):
            f0 = pick[line(g * group + 2 * p), :]
            f1 = pick[line(g * group + 2 * p + 1), :]
            left = jnp.where(low, f0, pltpu.roll(f1, 4, 0))
            right = jnp.where(low, pltpu.roll(f0, 4, 0), f1)
            x = jnp.concatenate([left, right], axis=1).astype(jnp.bfloat16)
            s = jnp.dot(x, turned[p], preferred_element_type=jnp.float32)
            to[p] = jnp.concatenate([jnp.where(low, s[:, :samples], 0.0), jnp.where(low, 0.0, s[:, samples:])], axis=1)

    def spread(g, sampled):
        for p in range(pairs):
            a = jnp.dot(sampled[p].astype(jnp.bfloat16), weights(g, p), preferred_element_type=jnp.float32)
            left, right = a[:, :LANES], a[:, LANES:]
            ret[line(g * group + 2 * p), :] = jnp.where(low, left, pltpu.roll(right, 4, 0))
            ret[line(g * group + 2 * p + 1), :] = jnp.where(low, pltpu.roll(left, 4, 0), right)

    fetch(0).wait()
    turn(0, turn_a)

    def body(i, carry):
        g = 2 * i
        fetch(g + 1).wait()

        @pl.when(g + 2 < groups)
        def _():
            fetch(g + 2).wait()

        turn(g + 1, turn_b)
        sample(g, turn_a, samp_a)
        spread(jnp.maximum(g - 1, 0), samp_b)
        turn(jnp.minimum(g + 2, groups - 1), turn_a)
        sample(g + 1, turn_b, samp_b)
        spread(g, samp_a)
        return carry

    lax.fori_loop(0, groups // 2, body, 0)
    spread(groups - 1, samp_b)
    for d in range(devices):
        out_ref[d] = ret[pl.ds(d * lines, lines), :].astype(jnp.bfloat16)


def bins(line, fetched, blocks):
    devices, lines, _ = fetched.shape
    count, samples, cells = blocks.shape
    group = 16
    return pl.pallas_call(
        functools.partial(bins_kernel, group),
        in_specs=[whole(pltpu.SMEM), whole()] + [whole(pl.ANY)],
        out_specs=whole(),
        out_shape=jax.ShapeDtypeStruct((devices, lines, LANES), jnp.bfloat16),
        scratch_shapes=[pltpu.VMEM(blocks.shape, jnp.bfloat16)]
        + [pltpu.VMEM((group // 2, cells, 2 * samples), jnp.bfloat16)] * 2
        + [pltpu.VMEM((group // 2, SUB, 2 * samples), jnp.float32)] * 2
        + [pltpu.VMEM((devices * lines, LANES), jnp.float32)] * 2
        + [pltpu.SemaphoreType.DMA((count // group,))],
        compiler_params=params(50),
        name="bins",
    )(line, fetched, blocks)


def laplace_kernel(field_ref, above_ref, below_ref, left_ref, right_ref, out_ref):
    beacons, rows, cols = field_ref.shape
    row = lax.broadcasted_iota(jnp.int32, (rows, cols), 0)
    col = lax.broadcasted_iota(jnp.int32, (rows, cols), 1)
    above, below = above_ref[...].astype(jnp.float32), below_ref[...].astype(jnp.float32)
    sides = jnp.concatenate([left_ref[...].astype(jnp.float32), right_ref[...].astype(jnp.float32)], axis=0).T
    for k in range(beacons):
        x = field_ref[k]
        up = jnp.where(row == 0, above[k : k + 1, :], pltpu.roll(x, 1, 0))
        down = jnp.where(row == rows - 1, below[k : k + 1, :], pltpu.roll(x, rows - 1, 0))
        left = jnp.where(col == 0, sides[:, k : k + 1], pltpu.roll(x, 1, 1))
        right = jnp.where(col == cols - 1, sides[:, beacons + k : beacons + k + 1], pltpu.roll(x, cols - 1, 1))
        out_ref[k] = smooth_weight * (4.0 * x - (down + up + right + left))


def laplace(field, above, below, left, right):
    return pl.pallas_call(
        laplace_kernel,
        in_specs=[whole()] * 5,
        out_specs=whole(),
        out_shape=jax.ShapeDtypeStruct(field.shape, jnp.float32),
        compiler_params=params(8),
        name="laplace",
    )(field, above, below, left, right)


def image_kernel(wanted_ref, arrived_ref, smooth_ref, direction_ref, residual_ref, image_ref, stats_ref, *sums):
    devices, cap = wanted_ref.shape
    beacons, rows, cols = direction_ref.shape
    bands, groups = rows // TILE_SIDE, cols // LANES
    for total in sums:
        total[...] = jnp.zeros_like(total)

    def body(d, carry):
        for r in range(0, cap, 2):
            pair = arrived_ref[d, r * SUB : (r + 2) * SUB, :].astype(jnp.float32)
            for q in range(min(2, cap - r)):
                at = pl.ds(pl.multiple_of(wanted_ref[d, r + q], SUB), SUB)
                sums[(r + q) % len(sums)][at, :] += pair[q * SUB : (q + 1) * SUB]
        return carry

    lax.fori_loop(0, devices, body, 0, unroll=2)
    lines = []
    units = []
    for k in range(beacons):
        unit = jnp.zeros((SUB, LANES), jnp.float32)
        for g in range(groups):
            x = []
            for band in range(bands):
                for h in range(2):
                    at = pl.ds((band * groups + g) * SUB * SUB + h * beacons + k, SUB, stride=SUB)
                    x.append(sum(total[at, :] for total in sums))
            x = swap_chunks(jnp.stack(x)).reshape(rows, LANES)
            x = x + smooth_ref[k, :, g * LANES : (g + 1) * LANES]
            image_ref[k, :, g * LANES : (g + 1) * LANES] = x
            unit = jnp.maximum(unit, jnp.max(jnp.abs(x).reshape(bands * 2, SUB, LANES), axis=0))
        unit = jnp.maximum(unit, 1e-30)
        inverse = 1.0 / unit
        terms = [jnp.zeros((SUB, LANES), jnp.float32)] * 4
        for i in range(rows // SUB):
            for g in range(groups):
                at = (k, slice(i * SUB, (i + 1) * SUB), slice(g * LANES, (g + 1) * LANES))
                x, d, r = image_ref[at], direction_ref[at], residual_ref[at]
                scaled = x * inverse
                terms = [t + v for t, v in zip(terms, (r * r, d * x, r * scaled, scaled * scaled))]
        lines.append(terms)
        units.append(unit)
    largest = [jnp.max(unit, axis=(0, 1), keepdims=True) for unit in units]
    rows_of = []
    for q in range(4):
        for k in range(beacons):
            t = lines[k][q]
            if q >= 2:
                share = units[k] * (1.0 / largest[k])
                t = t * share if q == 2 else t * share * share
            rows_of.append(jnp.sum(t, axis=0, keepdims=True))
    for k in range(beacons):
        first = lax.broadcasted_iota(jnp.int32, (1, LANES), 1) == 0
        rows_of.append(jnp.where(first, largest[k], 0.0))
    rows_of.append(jnp.zeros((LANES - len(rows_of), LANES), jnp.float32))
    stats = jnp.sum(jnp.concatenate(rows_of, axis=0).T, axis=0, keepdims=True)
    stats_ref[...] = jnp.broadcast_to(stats, stats_ref.shape)


def image_of(wanted, arrived, smooth, direction, residual):
    beacons, rows, cols = direction.shape
    return pl.pallas_call(
        image_kernel,
        in_specs=[whole(pltpu.SMEM)] + [whole()] * 4,
        out_specs=[whole(), whole()],
        out_shape=[
            jax.ShapeDtypeStruct(direction.shape, jnp.float32),
            jax.ShapeDtypeStruct((wanted.shape[0], LANES), jnp.float32),
        ],
        scratch_shapes=[pltpu.VMEM((beacons * rows * cols // LANES, LANES), jnp.float32)] * 4,
        compiler_params=params(16),
        name="image",
    )(wanted, arrived, smooth, direction, residual)


def update_kernel(
    stats_ref, solution_ref, residual_ref, direction_ref, image_ref, sol_ref, res_ref, dir_ref, sol, res, dire, sems
):
    beacons = direction_ref.shape[0]
    stats = stats_ref[...]

    def column(x, q):
        return pltpu.roll(x, LANES - q * beacons, 1) if q else x

    total = jnp.sum(stats, axis=0, keepdims=True)
    total = jnp.broadcast_to(total, (SUB, LANES))
    alpha = total / column(total, 1)
    size = alpha[:1] * column(stats, 4)
    moved = jnp.sum(size * (size * column(stats, 3) - 2.0 * column(stats, 2)), axis=0, keepdims=True)
    beta = (total + moved) / total
    copies = []
    for k in range(beacons):
        a, b = alpha[:1, k : k + 1], beta[:1, k : k + 1]
        d = direction_ref[k]
        r = residual_ref[k] - a * image_ref[k]
        sol[k] = solution_ref[k] + a * d
        res[k] = r
        dire[k] = r + b * d
        for q, (held, out) in enumerate(((sol, sol_ref), (res, res_ref), (dire, dir_ref))):
            copies.append(pltpu.make_async_copy(held.at[k], out.at[k], sems.at[q, k]))
            copies[-1].start()
    for copy in copies:
        copy.wait()


def update(stats, solution, residual, direction, image):
    return pl.pallas_call(
        update_kernel,
        in_specs=[whole()] * 5,
        out_specs=[whole(pl.ANY)] * 3,
        out_shape=[jax.ShapeDtypeStruct(direction.shape, jnp.float32)] * 3,
        scratch_shapes=[pltpu.VMEM(direction.shape, jnp.float32)] * 3
        + [pltpu.SemaphoreType.DMA((3, direction.shape[0]))],
        compiler_params=params(16),
        name="update",
    )(stats, solution, residual, direction, image)


def exchange(x):
    return lax.all_to_all(x, AXES, split_axis=0, concat_axis=0, tiled=True)


def shift(x, axis, step):
    size = lax.axis_size(axis)
    return lax.ppermute(x, axis, [(i, i + step) for i in range(size) if 0 <= i + step < size])


def per_device(solution, residual, direction, blocks, bin_owner, bin_tile):
    devices = lax.axis_size("tx") * lax.axis_size("ty")
    count = blocks.shape[0]
    cap = max(2, 3 * count // (2 * devices))
    lines = -(-cap // 2) * 2 * SUB

    line, request = prep(bin_owner.reshape(1, count), bin_tile.reshape(1, count), devices, cap, lines)
    wanted = exchange(request)
    own, top, bottom, sides = tiles(direction)
    above, below = shift(bottom, "tx", 1), shift(top, "tx", -1)
    beacons = direction.shape[0]
    left, right = shift(sides[:beacons], "ty", 1), shift(sides[beacons:], "ty", -1)
    smooth = laplace(direction, above, below, left, right)
    fetched = exchange(gather(wanted, own, lines))
    arrived = exchange(bins(line, fetched, blocks))
    image, stats = image_of(wanted, arrived, smooth, direction, residual)
    return update(exchange(stats), solution, residual, direction, image)


def solution(mesh):
    placed = (
        P(None, "tx", "ty"),
        P(None, "tx", "ty"),
        P(None, "tx", "ty"),
        P(AXES, None, None),
        P(AXES, None),
        P(AXES),
    )
    return jax.shard_map(
        per_device,
        mesh=mesh,
        in_specs=placed,
        out_specs=(P(None, "tx", "ty"),) * 3,
        check_vma=False,
    )
```

```python
import functools

import jax
import jax.numpy as jnp
from jax import lax
from jax.experimental import pallas as pl
from jax.experimental.pallas import tpu as pltpu
from jax.sharding import PartitionSpec as P

TILE_SIDE = 16
LANES = 128
SUB = 8
smooth_weight = 0.25

AXES = ("tx", "ty")


def whole(memory=pltpu.VMEM):
    return pl.BlockSpec(memory_space=memory)


def params(mib):
    return pltpu.CompilerParams(vmem_limit_bytes=mib << 20)


def swap_chunks(blocks):
    row = lax.broadcasted_iota(jnp.int32, (SUB, LANES), 0)
    lane = lax.broadcasted_iota(jnp.int32, (SUB, LANES), 1)
    chunk, rest = lane // TILE_SIDE, lane % TILE_SIDE
    first = (chunk + row) % SUB * TILE_SIDE + rest
    second = (row - chunk + SUB) % SUB * TILE_SIDE + rest

    def swap(x):
        x = jnp.take_along_axis(x, first, axis=1)
        for s in (1, 2, 4):
            x = jnp.where((chunk & s) != 0, pltpu.roll(x, s, 0), x)
        return jnp.take_along_axis(x, second, axis=1)

    return [swap(x) for x in blocks]


def prep_kernel(step, both_ref, line_ref, request_ref):
    devices, bins = request_ref.shape[0], both_ref.shape[1]
    owner, tile = both_ref[:1], both_ref[1:]
    earlier = (
        lax.broadcasted_iota(jnp.int32, (bins, bins), 0) < lax.broadcasted_iota(jnp.int32, (bins, bins), 1)
    ).astype(jnp.bfloat16)
    member = (lax.broadcasted_iota(jnp.int32, (devices, bins), 0) == owner).astype(jnp.float32)
    member16 = member.astype(jnp.bfloat16)
    before = jnp.dot(member16, earlier, preferred_element_type=jnp.float32)
    rank = jnp.sum(before * member, axis=0, keepdims=True).astype(jnp.int32)
    line_ref[...] = owner * step + rank * SUB
    place = lax.broadcasted_iota(jnp.int32, (request_ref.shape[1], bins), 0) == rank
    named = jnp.where(place, tile, 0).astype(jnp.float32).astype(jnp.bfloat16)
    request = lax.dot_general(member16, named, (((1,), (1,)), ((), ())), preferred_element_type=jnp.float32)
    request_ref[...] = request.astype(jnp.int32) * SUB


def prep(both, devices, cap, lines):
    bins = both.shape[1]
    return pl.pallas_call(
        functools.partial(prep_kernel, lines),
        in_specs=[whole()],
        out_specs=[whole()] * 2,
        out_shape=[
            jax.ShapeDtypeStruct((1, bins), jnp.int32),
            jax.ShapeDtypeStruct((devices, cap), jnp.int32),
        ],
        compiler_params=params(4),
        name="prep",
    )(both)


def tiles_kernel(field_ref, out_ref, top_ref, bottom_ref, sides_ref):
    beacons, rows, cols = field_ref.shape
    bands, groups = rows // TILE_SIDE, cols // LANES
    for k in range(beacons):
        for g in range(groups):
            x = field_ref[k, :, g * LANES : (g + 1) * LANES].astype(jnp.bfloat16).astype(jnp.float32)
            x = swap_chunks([x[i * SUB : (i + 1) * SUB] for i in range(bands * 2)])
            for band in range(bands):
                for h in range(2):
                    at = (band * groups + g) * SUB * SUB + h * beacons + k
                    out_ref[pl.ds(at, SUB, stride=SUB), :] = x[band * 2 + h]
    top_ref[...] = field_ref[:, 0, :].astype(jnp.bfloat16)
    bottom_ref[...] = field_ref[:, rows - 1, :].astype(jnp.bfloat16)
    lane = lax.broadcasted_iota(jnp.int32, (rows, LANES), 1)
    ends = jnp.zeros((rows, LANES), jnp.float32)
    for k in range(beacons):
        ends = jnp.where(lane == k, field_ref[k, :, cols - 1 :], ends)
        ends = jnp.where(lane == beacons + k, field_ref[k, :, :1], ends)
    sides_ref[...] = ends.T[: 2 * beacons].astype(jnp.bfloat16)


def tiles(field):
    beacons, rows, cols = field.shape
    return pl.pallas_call(
        tiles_kernel,
        in_specs=[whole()],
        out_specs=[whole()] * 4,
        out_shape=[
            jax.ShapeDtypeStruct((beacons * rows * cols // LANES, LANES), jnp.float32),
            jax.ShapeDtypeStruct((beacons, cols), jnp.bfloat16),
            jax.ShapeDtypeStruct((beacons, cols), jnp.bfloat16),
            jax.ShapeDtypeStruct((2 * beacons, rows), jnp.bfloat16),
        ],
        compiler_params=params(8),
        name="tiles",
    )(field)


def gather_kernel(wanted_ref, tiles_ref, out_ref):
    devices, cap = wanted_ref.shape

    def at(d, r):
        return tiles_ref[pl.ds(pl.multiple_of(wanted_ref[d, r], SUB), SUB), :]

    def body(d, carry):
        for r in range(0, cap - 1, 2):
            pair = jnp.concatenate([at(d, r), at(d, r + 1)], axis=0)
            out_ref[d, r * SUB : (r + 2) * SUB, :] = pair.astype(jnp.bfloat16)
        if cap % 2:
            pair = jnp.concatenate([at(d, cap - 1), jnp.zeros((SUB, LANES), jnp.float32)], axis=0)
            out_ref[d, (cap - 1) * SUB : (cap + 1) * SUB, :] = pair.astype(jnp.bfloat16)
        return carry

    lax.fori_loop(0, devices, body, 0, unroll=4)


def gather(wanted, own, lines):
    devices = wanted.shape[0]
    return pl.pallas_call(
        gather_kernel,
        in_specs=[whole(pltpu.SMEM), whole()],
        out_specs=whole(),
        out_shape=jax.ShapeDtypeStruct((devices, lines, LANES), jnp.bfloat16),
        compiler_params=params(8),
        name="gather",
    )(wanted, own)


def bins_kernel(
    group, line_ref, fetched_ref, blocks_ref, out_ref, held_ref, turn_a, turn_b, samp_a, samp_b, pick, ret, sems
):
    devices, lines, _ = fetched_ref.shape
    count, samples, cells = blocks_ref.shape
    groups, pairs = count // group, group // 2

    def fetch(i):
        part = pl.ds(i * group, group)
        return pltpu.make_async_copy(blocks_ref.at[part], held_ref.at[part], sems.at[i])

    for i in range(groups):
        fetch(i).start()
    for d in range(devices):
        pick[pl.ds(d * lines, lines), :] = fetched_ref[d].astype(jnp.float32)
        ret[pl.ds(d * lines, lines), :] = jnp.zeros((lines, LANES), jnp.float32)
    samp_b[...] = jnp.zeros_like(samp_b)
    low = lax.broadcasted_iota(jnp.int32, (SUB, LANES), 0) < 4

    def weights(g, p):
        return held_ref[pl.ds(g * group + 2 * p, 2)].reshape(2 * samples, cells)

    def turn(g, to):
        for p in range(pairs):
            to[p] = weights(g, p).T

    def line(b):
        return pl.ds(pl.multiple_of(line_ref[0, b], SUB), SUB)

    def sample(g, turned, to):
        for p in range(pairs):
            f0 = pick[line(g * group + 2 * p), :]
            f1 = pick[line(g * group + 2 * p + 1), :]
            left = jnp.where(low, f0, pltpu.roll(f1, 4, 0))
            right = jnp.where(low, pltpu.roll(f0, 4, 0), f1)
            x = jnp.concatenate([left, right], axis=1).astype(jnp.bfloat16)
            s = jnp.dot(x, turned[p], preferred_element_type=jnp.float32)
            to[p] = jnp.concatenate([jnp.where(low, s[:, :samples], 0.0), jnp.where(low, 0.0, s[:, samples:])], axis=1)

    def spread(g, sampled):
        for p in range(pairs):
            a = jnp.dot(sampled[p].astype(jnp.bfloat16), weights(g, p), preferred_element_type=jnp.float32)
            left, right = a[:, :LANES], a[:, LANES:]
            ret[line(g * group + 2 * p), :] = jnp.where(low, left, pltpu.roll(right, 4, 0))
            ret[line(g * group + 2 * p + 1), :] = jnp.where(low, pltpu.roll(left, 4, 0), right)

    fetch(0).wait()
    turn(0, turn_a)

    def body(i, carry):
        g = 2 * i
        fetch(g + 1).wait()

        @pl.when(g + 2 < groups)
        def _():
            fetch(g + 2).wait()

        turn(g + 1, turn_b)
        sample(g, turn_a, samp_a)
        spread(jnp.maximum(g - 1, 0), samp_b)
        turn(jnp.minimum(g + 2, groups - 1), turn_a)
        sample(g + 1, turn_b, samp_b)
        spread(g, samp_a)
        return carry

    lax.fori_loop(0, groups // 2, body, 0)
    spread(groups - 1, samp_b)
    for d in range(devices):
        out_ref[d] = ret[pl.ds(d * lines, lines), :].astype(jnp.bfloat16)


def bins(line, fetched, blocks):
    devices, lines, _ = fetched.shape
    count, samples, cells = blocks.shape
    group = 16
    return pl.pallas_call(
        functools.partial(bins_kernel, group),
        in_specs=[whole(pltpu.SMEM), whole()] + [whole(pl.ANY)],
        out_specs=whole(),
        out_shape=jax.ShapeDtypeStruct((devices, lines, LANES), jnp.bfloat16),
        scratch_shapes=[pltpu.VMEM(blocks.shape, jnp.bfloat16)]
        + [pltpu.VMEM((group // 2, cells, 2 * samples), jnp.bfloat16)] * 2
        + [pltpu.VMEM((group // 2, SUB, 2 * samples), jnp.float32)] * 2
        + [pltpu.VMEM((devices * lines, LANES), jnp.float32)] * 2
        + [pltpu.SemaphoreType.DMA((count // group,))],
        compiler_params=params(50),
        name="bins",
    )(line, fetched, blocks)


def laplace_kernel(field_ref, above_ref, below_ref, left_ref, right_ref, out_ref):
    beacons, rows, cols = field_ref.shape
    row = lax.broadcasted_iota(jnp.int32, (rows, cols), 0)
    col = lax.broadcasted_iota(jnp.int32, (rows, cols), 1)
    above, below = above_ref[...].astype(jnp.float32), below_ref[...].astype(jnp.float32)
    sides = jnp.concatenate([left_ref[...].astype(jnp.float32), right_ref[...].astype(jnp.float32)], axis=0).T
    for k in range(beacons):
        x = field_ref[k]
        up = jnp.where(row == 0, above[k : k + 1, :], pltpu.roll(x, 1, 0))
        down = jnp.where(row == rows - 1, below[k : k + 1, :], pltpu.roll(x, rows - 1, 0))
        left = jnp.where(col == 0, sides[:, k : k + 1], pltpu.roll(x, 1, 1))
        right = jnp.where(col == cols - 1, sides[:, beacons + k : beacons + k + 1], pltpu.roll(x, cols - 1, 1))
        out_ref[k] = smooth_weight * (4.0 * x - (down + up + right + left))


def laplace(field, above, below, left, right):
    return pl.pallas_call(
        laplace_kernel,
        in_specs=[whole()] * 5,
        out_specs=whole(),
        out_shape=jax.ShapeDtypeStruct(field.shape, jnp.float32),
        compiler_params=params(8),
        name="laplace",
    )(field, above, below, left, right)


def image_kernel(wanted_ref, arrived_ref, smooth_ref, direction_ref, residual_ref, image_ref, stats_ref, *sums):
    devices, cap = wanted_ref.shape
    beacons, rows, cols = direction_ref.shape
    bands, groups = rows // TILE_SIDE, cols // LANES
    for total in sums:
        total[...] = jnp.zeros_like(total)

    def body(d, carry):
        for r in range(0, cap, 2):
            pair = arrived_ref[d, r * SUB : (r + 2) * SUB, :].astype(jnp.float32)
            for q in range(min(2, cap - r)):
                at = pl.ds(pl.multiple_of(wanted_ref[d, r + q], SUB), SUB)
                sums[(r + q) % len(sums)][at, :] += pair[q * SUB : (q + 1) * SUB]
        return carry

    lax.fori_loop(0, devices, body, 0, unroll=2)
    lines = []
    units = []
    for k in range(beacons):
        unit = jnp.zeros((SUB, LANES), jnp.float32)
        for g in range(groups):
            x = []
            for band in range(bands):
                for h in range(2):
                    at = pl.ds((band * groups + g) * SUB * SUB + h * beacons + k, SUB, stride=SUB)
                    x.append(sum(total[at, :] for total in sums))
            x = jnp.concatenate(swap_chunks(x), axis=0)
            x = x + smooth_ref[k, :, g * LANES : (g + 1) * LANES]
            image_ref[k, :, g * LANES : (g + 1) * LANES] = x
            unit = jnp.maximum(unit, jnp.max(jnp.abs(x).reshape(bands * 2, SUB, LANES), axis=0))
        unit = jnp.maximum(unit, 1e-30)
        inverse = 1.0 / unit
        terms = [jnp.zeros((SUB, LANES), jnp.float32)] * 4
        for i in range(rows // SUB):
            for g in range(groups):
                at = (k, slice(i * SUB, (i + 1) * SUB), slice(g * LANES, (g + 1) * LANES))
                x, d, r = image_ref[at], direction_ref[at], residual_ref[at]
                scaled = x * inverse
                terms = [t + v for t, v in zip(terms, (r * r, d * x, r * scaled, scaled * scaled))]
        lines.append(terms)
        units.append(unit)
    largest = [jnp.max(unit, axis=(0, 1), keepdims=True) for unit in units]
    rows_of = []
    for q in range(4):
        for k in range(beacons):
            t = lines[k][q]
            if q >= 2:
                share = units[k] * (1.0 / largest[k])
                t = t * share if q == 2 else t * share * share
            rows_of.append(jnp.sum(t, axis=0, keepdims=True))
    for k in range(beacons):
        first = lax.broadcasted_iota(jnp.int32, (1, LANES), 1) == 0
        rows_of.append(jnp.where(first, largest[k], 0.0))
    rows_of.append(jnp.zeros((LANES - len(rows_of), LANES), jnp.float32))
    stats = jnp.sum(jnp.concatenate(rows_of, axis=0).T, axis=0, keepdims=True)
    stats_ref[...] = jnp.broadcast_to(stats, stats_ref.shape)


def image_of(wanted, arrived, smooth, direction, residual):
    beacons, rows, cols = direction.shape
    return pl.pallas_call(
        image_kernel,
        in_specs=[whole(pltpu.SMEM)] + [whole()] * 4,
        out_specs=[whole(), whole()],
        out_shape=[
            jax.ShapeDtypeStruct(direction.shape, jnp.float32),
            jax.ShapeDtypeStruct((wanted.shape[0], LANES), jnp.float32),
        ],
        scratch_shapes=[pltpu.VMEM((beacons * rows * cols // LANES, LANES), jnp.float32)] * 4,
        compiler_params=params(16),
        name="image",
    )(wanted, arrived, smooth, direction, residual)


def update_kernel(
    stats_ref, solution_ref, residual_ref, direction_ref, image_ref, sol_ref, res_ref, dir_ref, sol, res, dire, sems
):
    beacons = direction_ref.shape[0]
    stats = stats_ref[...]

    def column(x, q):
        return pltpu.roll(x, LANES - q * beacons, 1) if q else x

    total = jnp.sum(stats, axis=0, keepdims=True)
    total = jnp.broadcast_to(total, (SUB, LANES))
    alpha = total / column(total, 1)
    size = alpha[:1] * column(stats, 4)
    moved = jnp.sum(size * (size * column(stats, 3) - 2.0 * column(stats, 2)), axis=0, keepdims=True)
    beta = (total + moved) / total
    copies = []
    for k in range(beacons):
        a, b = alpha[:1, k : k + 1], beta[:1, k : k + 1]
        d = direction_ref[k]
        r = residual_ref[k] - a * image_ref[k]
        sol[k] = solution_ref[k] + a * d
        res[k] = r
        dire[k] = r + b * d
        for q, (held, out) in enumerate(((sol, sol_ref), (res, res_ref), (dire, dir_ref))):
            copies.append(pltpu.make_async_copy(held.at[k], out.at[k], sems.at[q, k]))
            copies[-1].start()
    for copy in copies:
        copy.wait()


def update(stats, solution, residual, direction, image):
    return pl.pallas_call(
        update_kernel,
        in_specs=[whole()] * 5,
        out_specs=[whole(pl.ANY)] * 3,
        out_shape=[jax.ShapeDtypeStruct(direction.shape, jnp.float32)] * 3,
        scratch_shapes=[pltpu.VMEM(direction.shape, jnp.float32)] * 3
        + [pltpu.SemaphoreType.DMA((3, direction.shape[0]))],
        compiler_params=params(16),
        name="update",
    )(stats, solution, residual, direction, image)


def exchange(x):
    return lax.all_to_all(x, AXES, split_axis=0, concat_axis=0, tiled=True)


def shift(x, axis, step):
    size = lax.axis_size(axis)
    return lax.ppermute(x, axis, [(i, i + step) for i in range(size) if 0 <= i + step < size])


def per_device(solution, residual, direction, blocks, bin_owner, bin_tile):
    devices = lax.axis_size("tx") * lax.axis_size("ty")
    count = blocks.shape[0]
    cap = max(2, 3 * count // (2 * devices))
    lines = -(-cap // 2) * 2 * SUB

    both = jnp.concatenate([bin_owner.reshape(1, count), bin_tile.reshape(1, count)], axis=0)
    line, request = prep(both, devices, cap, lines)
    wanted = exchange(request)
    own, top, bottom, sides = tiles(direction)
    above, below = shift(bottom, "tx", 1), shift(top, "tx", -1)
    beacons = direction.shape[0]
    left, right = shift(sides[:beacons], "ty", 1), shift(sides[beacons:], "ty", -1)
    smooth = laplace(direction, above, below, left, right)
    fetched = exchange(gather(wanted, own, lines))
    arrived = exchange(bins(line, fetched, blocks))
    image, stats = image_of(wanted, arrived, smooth, direction, residual)
    return update(exchange(stats), solution, residual, direction, image)


def solution(mesh):
    placed = (
        P(None, "tx", "ty"),
        P(None, "tx", "ty"),
        P(None, "tx", "ty"),
        P(AXES, None, None),
        P(AXES, None),
        P(AXES),
    )
    return jax.shard_map(
        per_device,
        mesh=mesh,
        in_specs=placed,
        out_specs=(P(None, "tx", "ty"),) * 3,
        check_vma=False,
    )
```

```python
import functools

import jax
import jax.numpy as jnp
from jax import lax
from jax.experimental import pallas as pl
from jax.experimental.pallas import tpu as pltpu
from jax.sharding import PartitionSpec as P

TILE_SIDE = 16
LANES = 128
SUB = 8
smooth_weight = 0.25

TY = ("th", "tl")
AXES = ("tx", "th", "tl")
HALF = ("tx", "tl")


def whole(memory=pltpu.VMEM):
    return pl.BlockSpec(memory_space=memory)


def params(mib):
    return pltpu.CompilerParams(vmem_limit_bytes=mib << 20)


def swap_chunks(blocks):
    row = lax.broadcasted_iota(jnp.int32, (SUB, LANES), 0)
    lane = lax.broadcasted_iota(jnp.int32, (SUB, LANES), 1)
    chunk, rest = lane // TILE_SIDE, lane % TILE_SIDE
    first = (chunk + row) % SUB * TILE_SIDE + rest
    second = (row - chunk + SUB) % SUB * TILE_SIDE + rest

    def swap(x):
        x = jnp.take_along_axis(x, first, axis=1)
        for s in (1, 2, 4):
            x = jnp.where((chunk & s) != 0, pltpu.roll(x, s, 0), x)
        return jnp.take_along_axis(x, second, axis=1)

    return [swap(x) for x in blocks]


def prep_kernel(step, span, tiles, both_ref, line_ref, request_ref):
    devices, bins = request_ref.shape[0], both_ref.shape[1]
    owner, tile = both_ref[:1], both_ref[1:]
    column = lax.rem(owner, 2 * span)
    far = (lax.div(column, span) != lax.axis_index("th")).astype(jnp.int32)
    place = (lax.div(owner, 2 * span) * span + lax.rem(column, span)) * 2 + far
    earlier = (
        lax.broadcasted_iota(jnp.int32, (bins, bins), 0) < lax.broadcasted_iota(jnp.int32, (bins, bins), 1)
    ).astype(jnp.bfloat16)
    member = (lax.broadcasted_iota(jnp.int32, (devices, bins), 0) == place).astype(jnp.float32)
    member16 = member.astype(jnp.bfloat16)
    before = jnp.dot(member16, earlier, preferred_element_type=jnp.float32)
    rank = jnp.sum(before * member, axis=0, keepdims=True).astype(jnp.int32)
    line_ref[:1] = place * step + rank * SUB
    line_ref[1:] = owner * step + rank * SUB
    at = lax.broadcasted_iota(jnp.int32, (request_ref.shape[1], bins), 0) == rank
    named = jnp.where(at, tile + far * tiles, 0).astype(jnp.float32).astype(jnp.bfloat16)
    request = lax.dot_general(member16, named, (((1,), (1,)), ((), ())), preferred_element_type=jnp.float32)
    request_ref[...] = request.astype(jnp.int32) * SUB


def prep(both, devices, cap, lines, span, tiles):
    bins = both.shape[1]
    return pl.pallas_call(
        functools.partial(prep_kernel, lines, span, tiles),
        in_specs=[whole()],
        out_specs=[whole()] * 2,
        out_shape=[
            jax.ShapeDtypeStruct((2, bins), jnp.int32),
            jax.ShapeDtypeStruct((devices, cap), jnp.int32),
        ],
        compiler_params=params(4),
        name="prep",
    )(both)


def tiles_kernel(field_ref, out_ref, top_ref, bottom_ref, sides_ref, held):
    beacons, rows, cols = field_ref.shape
    bands, groups = rows // TILE_SIDE, cols // LANES
    for k in range(beacons):
        for g in range(groups):
            x = field_ref[k, :, g * LANES : (g + 1) * LANES]
            x = swap_chunks([x[i * SUB : (i + 1) * SUB] for i in range(bands * 2)])
            for band in range(bands):
                for h in range(2):
                    at = (band * groups + g) * SUB * SUB + h * beacons + k
                    held[pl.ds(at, SUB, stride=SUB), :] = x[band * 2 + h]
    out_ref[...] = held[...].astype(jnp.bfloat16)
    top_ref[...] = field_ref[:, 0, :].astype(jnp.bfloat16)
    bottom_ref[...] = field_ref[:, rows - 1, :].astype(jnp.bfloat16)
    lane = lax.broadcasted_iota(jnp.int32, (rows, LANES), 1)
    ends = jnp.zeros((rows, LANES), jnp.float32)
    for k in range(beacons):
        ends = jnp.where(lane == k, field_ref[k, :, cols - 1 :], ends)
        ends = jnp.where(lane == beacons + k, field_ref[k, :, :1], ends)
    sides_ref[...] = ends.T[: 2 * beacons].astype(jnp.bfloat16)


def tiles(field):
    beacons, rows, cols = field.shape
    return pl.pallas_call(
        tiles_kernel,
        in_specs=[whole()],
        out_specs=[whole()] * 4,
        out_shape=[
            jax.ShapeDtypeStruct((beacons * rows * cols // LANES, LANES), jnp.bfloat16),
            jax.ShapeDtypeStruct((beacons, cols), jnp.bfloat16),
            jax.ShapeDtypeStruct((beacons, cols), jnp.bfloat16),
            jax.ShapeDtypeStruct((2 * beacons, rows), jnp.bfloat16),
        ],
        scratch_shapes=[pltpu.VMEM((beacons * rows * cols // LANES, LANES), jnp.float32)],
        compiler_params=params(8),
        name="tiles",
    )(field)


def gather_kernel(cap, wanted_ref, own_ref, other_ref, *rest):
    *after, out_ref, held = rest
    peers, lines = wanted_ref.shape[0], out_ref.shape[1] // 2
    rows = own_ref.shape[0]
    held[:rows] = own_ref[...].astype(jnp.float32)
    held[rows:] = other_ref[...].astype(jnp.float32)

    def at(d, r):
        return held[pl.ds(pl.multiple_of(wanted_ref[d, r], SUB), SUB), :]

    def body(d, carry):
        for block in range(2):
            for r in range(0, cap, 2):
                to = block * lines + r * SUB
                one = at(d, block * cap + r)
                two = at(d, block * cap + r + 1) if r + 1 < cap else jnp.zeros_like(one)
                out_ref[d, to : to + 2 * SUB, :] = jnp.concatenate([one, two], axis=0).astype(jnp.bfloat16)
        return carry

    lax.fori_loop(0, peers, body, 0, unroll=2)


def gather(wanted, own, other, lines, *after):
    peers = wanted.shape[0]
    return pl.pallas_call(
        functools.partial(gather_kernel, wanted.shape[1] // 2),
        in_specs=[whole(pltpu.SMEM), whole(), whole()] + [whole(pl.ANY)] * len(after),
        out_specs=whole(),
        out_shape=jax.ShapeDtypeStruct((peers, 2 * lines, LANES), jnp.bfloat16),
        scratch_shapes=[pltpu.VMEM((2 * own.shape[0], LANES), jnp.float32)],
        compiler_params=params(8),
        name="gather",
    )(wanted, own, other, *after)


def bins_kernel(
    group, line_ref, fetched_ref, blocks_ref, out_ref, held_ref, turn_a, turn_b, samp_a, samp_b, pick, ret, sems
):
    devices, lines, _ = fetched_ref.shape
    count, samples, cells = blocks_ref.shape
    groups, pairs = count // group, group // 2

    def fetch(i):
        part = pl.ds(i * group, group)
        return pltpu.make_async_copy(blocks_ref.at[part], held_ref.at[part], sems.at[i])

    for i in range(groups):
        fetch(i).start()
    for d in range(devices):
        pick[pl.ds(d * lines, lines), :] = fetched_ref[d].astype(jnp.float32)
        ret[pl.ds(d * lines, lines), :] = jnp.zeros((lines, LANES), jnp.float32)
    samp_b[...] = jnp.zeros_like(samp_b)
    low = lax.broadcasted_iota(jnp.int32, (SUB, LANES), 0) < 4

    def weights(g, p):
        return held_ref[pl.ds(g * group + 2 * p, 2)].reshape(2 * samples, cells)

    def turn(g, to):
        for p in range(pairs):
            to[p] = weights(g, p).T

    def line(b, back):
        return pl.ds(pl.multiple_of(line_ref[back, b], SUB), SUB)

    def sample(g, turned, to):
        for p in range(pairs):
            f0 = pick[line(g * group + 2 * p, 0), :]
            f1 = pick[line(g * group + 2 * p + 1, 0), :]
            left = jnp.where(low, f0, pltpu.roll(f1, 4, 0))
            right = jnp.where(low, pltpu.roll(f0, 4, 0), f1)
            x = jnp.concatenate([left, right], axis=1).astype(jnp.bfloat16)
            s = jnp.dot(x, turned[p], preferred_element_type=jnp.float32)
            to[p] = jnp.concatenate([jnp.where(low, s[:, :samples], 0.0), jnp.where(low, 0.0, s[:, samples:])], axis=1)

    def spread(g, sampled):
        for p in range(pairs):
            a = jnp.dot(sampled[p].astype(jnp.bfloat16), weights(g, p), preferred_element_type=jnp.float32)
            left, right = a[:, :LANES], a[:, LANES:]
            ret[line(g * group + 2 * p, 1), :] = jnp.where(low, left, pltpu.roll(right, 4, 0))
            ret[line(g * group + 2 * p + 1, 1), :] = jnp.where(low, pltpu.roll(left, 4, 0), right)

    fetch(0).wait()
    turn(0, turn_a)

    def body(i, carry):
        g = 2 * i
        fetch(g + 1).wait()

        @pl.when(g + 2 < groups)
        def _():
            fetch(g + 2).wait()

        turn(g + 1, turn_b)
        sample(g, turn_a, samp_a)
        spread(jnp.maximum(g - 1, 0), samp_b)
        turn(jnp.minimum(g + 2, groups - 1), turn_a)
        sample(g + 1, turn_b, samp_b)
        spread(g, samp_a)
        return carry

    lax.fori_loop(0, groups // 2, body, 0)
    spread(groups - 1, samp_b)
    for d in range(devices):
        out_ref[d] = ret[pl.ds(d * lines, lines), :].astype(jnp.bfloat16)


def bins(line, fetched, blocks):
    devices, lines, _ = fetched.shape
    count, samples, cells = blocks.shape
    group = 16
    return pl.pallas_call(
        functools.partial(bins_kernel, group),
        in_specs=[whole(pltpu.SMEM), whole()] + [whole(pl.ANY)],
        out_specs=whole(),
        out_shape=jax.ShapeDtypeStruct((devices, lines, LANES), jnp.bfloat16),
        scratch_shapes=[pltpu.VMEM(blocks.shape, jnp.bfloat16)]
        + [pltpu.VMEM((group // 2, cells, 2 * samples), jnp.bfloat16)] * 2
        + [pltpu.VMEM((group // 2, SUB, 2 * samples), jnp.float32)] * 2
        + [pltpu.VMEM((devices * lines, LANES), jnp.float32)] * 2
        + [pltpu.SemaphoreType.DMA((count // group,))],
        compiler_params=params(50),
        name="bins",
    )(line, fetched, blocks)


def laplace_kernel(field_ref, above_ref, below_ref, left_ref, right_ref, out_ref):
    beacons, rows, cols = field_ref.shape
    row = lax.broadcasted_iota(jnp.int32, (rows, cols), 0)
    col = lax.broadcasted_iota(jnp.int32, (rows, cols), 1)
    above, below = above_ref[...].astype(jnp.float32), below_ref[...].astype(jnp.float32)
    sides = jnp.concatenate([left_ref[...].astype(jnp.float32), right_ref[...].astype(jnp.float32)], axis=0).T
    for k in range(beacons):
        x = field_ref[k]
        up = jnp.where(row == 0, above[k : k + 1, :], pltpu.roll(x, 1, 0))
        down = jnp.where(row == rows - 1, below[k : k + 1, :], pltpu.roll(x, rows - 1, 0))
        left = jnp.where(col == 0, sides[:, k : k + 1], pltpu.roll(x, 1, 1))
        right = jnp.where(col == cols - 1, sides[:, beacons + k : beacons + k + 1], pltpu.roll(x, cols - 1, 1))
        out_ref[k] = smooth_weight * (4.0 * x - (down + up + right + left))


def laplace(field, above, below, left, right):
    return pl.pallas_call(
        laplace_kernel,
        in_specs=[whole()] * 5,
        out_specs=whole(),
        out_shape=jax.ShapeDtypeStruct(field.shape, jnp.float32),
        compiler_params=params(8),
        name="laplace",
    )(field, above, below, left, right)


def image_kernel(near_ref, far_ref, arrived_ref, smooth_ref, direction_ref, residual_ref, image_ref, stats_ref, *sums):
    peers, cap = near_ref.shape[0], near_ref.shape[1] // 2
    beacons, rows, cols = direction_ref.shape
    bands, groups = rows // TILE_SIDE, cols // LANES
    span = lax.axis_size("tl")
    half = lax.axis_index("th")
    for total in sums:
        total[...] = jnp.zeros_like(total)

    def body(q, carry):
        row, place = lax.div(q, span) * (2 * span), lax.rem(q, span)
        for away in range(2):
            d = row + (1 - half if away else half) * span + place
            for r in range(0, cap, 2):
                pair = arrived_ref[d, r * SUB : (r + 2) * SUB, :].astype(jnp.float32)
                for e in range(min(2, cap - r)):
                    first = far_ref[q, cap + r + e] - sums[0].shape[0] if away else near_ref[q, r + e]
                    if away:
                        first = jnp.maximum(first, 0)
                    at = pl.ds(pl.multiple_of(first, SUB), SUB)
                    sums[(r + e) % len(sums)][at, :] += pair[e * SUB : (e + 1) * SUB]
        return carry

    lax.fori_loop(0, peers, body, 0)
    lines = []
    units = []
    for k in range(beacons):
        unit = jnp.zeros((SUB, LANES), jnp.float32)
        for g in range(groups):
            x = []
            for band in range(bands):
                for h in range(2):
                    at = pl.ds((band * groups + g) * SUB * SUB + h * beacons + k, SUB, stride=SUB)
                    x.append(sum(total[at, :] for total in sums))
            x = jnp.concatenate(swap_chunks(x), axis=0)
            x = x + smooth_ref[k, :, g * LANES : (g + 1) * LANES]
            image_ref[k, :, g * LANES : (g + 1) * LANES] = x
            unit = jnp.maximum(unit, jnp.max(jnp.abs(x).reshape(bands * 2, SUB, LANES), axis=0))
        unit = jnp.maximum(unit, 1e-30)
        inverse = 1.0 / unit
        terms = [jnp.zeros((SUB, LANES), jnp.float32)] * 4
        for i in range(rows // SUB):
            for g in range(groups):
                at = (k, slice(i * SUB, (i + 1) * SUB), slice(g * LANES, (g + 1) * LANES))
                x, d, r = image_ref[at], direction_ref[at], residual_ref[at]
                scaled = x * inverse
                terms = [t + v for t, v in zip(terms, (r * r, d * x, r * scaled, scaled * scaled))]
        lines.append(terms)
        units.append(unit)
    largest = [jnp.max(unit, axis=(0, 1), keepdims=True) for unit in units]
    rows_of = []
    for q in range(4):
        for k in range(beacons):
            t = lines[k][q]
            if q >= 2:
                share = units[k] * (1.0 / largest[k])
                t = t * share if q == 2 else t * share * share
            rows_of.append(jnp.sum(t, axis=0, keepdims=True))
    for k in range(beacons):
        first = lax.broadcasted_iota(jnp.int32, (1, LANES), 1) == 0
        rows_of.append(jnp.where(first, largest[k], 0.0))
    rows_of.append(jnp.zeros((LANES - len(rows_of), LANES), jnp.float32))
    stats = jnp.sum(jnp.concatenate(rows_of, axis=0).T, axis=0, keepdims=True)
    stats_ref[...] = jnp.broadcast_to(stats, stats_ref.shape)


def image_of(near, far, arrived, smooth, direction, residual):
    beacons, rows, cols = direction.shape
    return pl.pallas_call(
        image_kernel,
        in_specs=[whole(pltpu.SMEM)] * 2 + [whole()] * 4,
        out_specs=[whole(), whole()],
        out_shape=[
            jax.ShapeDtypeStruct(direction.shape, jnp.float32),
            jax.ShapeDtypeStruct((arrived.shape[0], LANES), jnp.float32),
        ],
        scratch_shapes=[pltpu.VMEM((beacons * rows * cols // LANES, LANES), jnp.float32)] * 4,
        compiler_params=params(16),
        name="image",
    )(near, far, arrived, smooth, direction, residual)


def update_kernel(
    stats_ref, solution_ref, residual_ref, direction_ref, image_ref, sol_ref, res_ref, dir_ref, sol, res, dire, sems
):
    beacons = direction_ref.shape[0]
    stats = stats_ref[...]

    def column(x, q):
        return pltpu.roll(x, LANES - q * beacons, 1) if q else x

    total = jnp.sum(stats, axis=0, keepdims=True)
    total = jnp.broadcast_to(total, (SUB, LANES))
    alpha = total / column(total, 1)
    size = alpha[:1] * column(stats, 4)
    moved = jnp.sum(size * (size * column(stats, 3) - 2.0 * column(stats, 2)), axis=0, keepdims=True)
    beta = (total + moved) / total
    copies = []
    for k in range(beacons):
        a, b = alpha[:1, k : k + 1], beta[:1, k : k + 1]
        d = direction_ref[k]
        r = residual_ref[k] - a * image_ref[k]
        sol[k] = solution_ref[k] + a * d
        res[k] = r
        dire[k] = r + b * d
        for q, (held, out) in enumerate(((sol, sol_ref), (res, res_ref), (dire, dir_ref))):
            copies.append(pltpu.make_async_copy(held.at[k], out.at[k], sems.at[q, k]))
            copies[-1].start()
    for copy in copies:
        copy.wait()


def update(stats, solution, residual, direction, image):
    return pl.pallas_call(
        update_kernel,
        in_specs=[whole()] * 5,
        out_specs=[whole(pl.ANY)] * 3,
        out_shape=[jax.ShapeDtypeStruct(direction.shape, jnp.float32)] * 3,
        scratch_shapes=[pltpu.VMEM(direction.shape, jnp.float32)] * 3
        + [pltpu.SemaphoreType.DMA((3, direction.shape[0]))],
        compiler_params=params(16),
        name="update",
    )(stats, solution, residual, direction, image)


def exchange(x, axes):
    return lax.all_to_all(x, axes, split_axis=0, concat_axis=0, tiled=True)


def shift(x, axis, step):
    size = lax.axis_size(axis)
    return lax.ppermute(x, axis, [(i, i + step) for i in range(size) if 0 <= i + step < size])


def trade(x):
    return lax.ppermute(x, "th", [(0, 1), (1, 0)])


def per_device(solution, residual, direction, blocks, bin_owner, bin_tile):
    devices, span = lax.axis_size(AXES), lax.axis_size("tl")
    count = blocks.shape[0]
    cap = max(2, 3 * count // (2 * devices))
    lines = -(-cap // 2) * 2 * SUB
    beacons, rows, cols = direction.shape

    own, top, bottom, sides = tiles(direction)
    other = trade(own)
    both = jnp.concatenate([bin_owner.reshape(1, count), bin_tile.reshape(1, count)], axis=0)
    line, request = prep(both, devices, cap, lines, span, rows * cols // TILE_SIDE**2)
    near = exchange(request.reshape(devices // 2, 2 * cap), HALF)
    far = trade(near)
    above, below = shift(bottom, "tx", 1), shift(top, "tx", -1)
    left, right = shift(sides[:beacons], TY, 1), shift(sides[beacons:], TY, -1)
    smooth = laplace(direction, above, below, left, right)
    fetched = exchange(gather(near, own, other, lines, far), HALF).reshape(devices, lines, LANES)
    arrived = exchange(bins(line, fetched, blocks), AXES)
    image, stats = image_of(near, far, arrived, smooth, direction, residual)
    return update(exchange(stats, AXES), solution, residual, direction, image)


def solution(mesh):
    rows, cols = mesh.devices.shape
    halves = jax.sharding.Mesh(mesh.devices.reshape(rows, 2, cols // 2), AXES)
    field = P(None, "tx", TY)
    return jax.shard_map(
        per_device,
        mesh=halves,
        in_specs=(field, field, field, P(AXES, None, None), P(AXES, None), P(AXES)),
        out_specs=(field,) * 3,
        check_vma=False,
    )
```

```python
import functools

import jax
import jax.numpy as jnp
from jax import lax
from jax.experimental import pallas as pl
from jax.experimental.pallas import tpu as pltpu
from jax.sharding import PartitionSpec as P

TILE_SIDE = 16
LANES = 128
SUB = 8
smooth_weight = 0.25

TY = ("th", "tl")
AXES = ("tx", "th", "tl")
HALF = ("tx", "tl")


def whole(memory=pltpu.VMEM):
    return pl.BlockSpec(memory_space=memory)


def params(mib):
    return pltpu.CompilerParams(vmem_limit_bytes=mib << 20)


def swap_chunks(blocks):
    row = lax.broadcasted_iota(jnp.int32, (SUB, LANES), 0)
    lane = lax.broadcasted_iota(jnp.int32, (SUB, LANES), 1)
    chunk, rest = lane // TILE_SIDE, lane % TILE_SIDE
    first = (chunk + row) % SUB * TILE_SIDE + rest
    second = (row - chunk + SUB) % SUB * TILE_SIDE + rest

    def swap(x):
        x = jnp.take_along_axis(x, first, axis=1)
        for s in (1, 2, 4):
            x = jnp.where((chunk & s) != 0, pltpu.roll(x, s, 0), x)
        return jnp.take_along_axis(x, second, axis=1)

    return [swap(x) for x in blocks]


def prep_kernel(step, span, tiles, both_ref, line_ref, request_ref):
    devices, bins = request_ref.shape[0], both_ref.shape[1]
    owner, tile = both_ref[:1], both_ref[1:]
    column = lax.rem(owner, 2 * span)
    far = (lax.div(column, span) != lax.axis_index("th")).astype(jnp.int32)
    place = (lax.div(owner, 2 * span) * span + lax.rem(column, span)) * 2 + far
    earlier = (
        lax.broadcasted_iota(jnp.int32, (bins, bins), 0) < lax.broadcasted_iota(jnp.int32, (bins, bins), 1)
    ).astype(jnp.bfloat16)
    member = (lax.broadcasted_iota(jnp.int32, (devices, bins), 0) == place).astype(jnp.float32)
    member16 = member.astype(jnp.bfloat16)
    before = jnp.dot(member16, earlier, preferred_element_type=jnp.float32)
    rank = jnp.sum(before * member, axis=0, keepdims=True).astype(jnp.int32)
    line_ref[:1] = place * step + rank * SUB
    line_ref[1:] = owner * step + rank * SUB
    at = lax.broadcasted_iota(jnp.int32, (request_ref.shape[1], bins), 0) == rank
    named = jnp.where(at, tile + far * tiles, 0).astype(jnp.float32).astype(jnp.bfloat16)
    request = lax.dot_general(member16, named, (((1,), (1,)), ((), ())), preferred_element_type=jnp.float32)
    request_ref[...] = request.astype(jnp.int32) * SUB


def prep(both, devices, cap, lines, span, tiles):
    bins = both.shape[1]
    return pl.pallas_call(
        functools.partial(prep_kernel, lines, span, tiles),
        in_specs=[whole()],
        out_specs=[whole()] * 2,
        out_shape=[
            jax.ShapeDtypeStruct((2, bins), jnp.int32),
            jax.ShapeDtypeStruct((devices, cap), jnp.int32),
        ],
        compiler_params=params(4),
        name="prep",
    )(both)


def tiles_kernel(field_ref, out_ref, edges_ref, copy_ref, held):
    beacons, rows, cols = field_ref.shape
    bands, groups = rows // TILE_SIDE, cols // LANES
    for k in range(beacons):
        for g in range(groups):
            x = field_ref[k, :, g * LANES : (g + 1) * LANES]
            x = swap_chunks([x[i * SUB : (i + 1) * SUB] for i in range(bands * 2)])
            for band in range(bands):
                for h in range(2):
                    at = (band * groups + g) * SUB * SUB + h * beacons + k
                    held[pl.ds(at, SUB, stride=SUB), :] = x[band * 2 + h]
    copy_ref[...] = field_ref[...]
    count = held.shape[0]
    out_ref[:count] = held[...].astype(jnp.bfloat16)
    ends = [field_ref[k, r : r + 1, g * LANES : (g + 1) * LANES] for r in (0, rows - 1) for k in range(beacons) for g in range(groups)]
    edges_ref[...] = jnp.concatenate(ends, axis=0).astype(jnp.bfloat16)
    lane = lax.broadcasted_iota(jnp.int32, (rows, LANES), 1)
    sides = jnp.zeros((rows, LANES), jnp.float32)
    for k in range(beacons):
        sides = jnp.where(lane == k, field_ref[k, :, cols - 1 :], sides)
        sides = jnp.where(lane == beacons + k, field_ref[k, :, :1], sides)
    out_ref[count:] = sides.T[: 2 * SUB].astype(jnp.bfloat16)


def tiles(field):
    beacons, rows, cols = field.shape
    return pl.pallas_call(
        tiles_kernel,
        in_specs=[whole()],
        out_specs=[whole()] * 3,
        out_shape=[
            jax.ShapeDtypeStruct((beacons * rows * cols // LANES + 2 * SUB, LANES), jnp.bfloat16),
            jax.ShapeDtypeStruct((2 * SUB, LANES), jnp.bfloat16),
            jax.ShapeDtypeStruct(field.shape, field.dtype),
        ],
        scratch_shapes=[pltpu.VMEM((beacons * rows * cols // LANES, LANES), jnp.float32)],
        compiler_params=params(8),
        name="tiles",
    )(field)


def gather_kernel(cap, wanted_ref, own_ref, other_ref, edges_ref, after_ref, out_ref, held):
    peers, lines = wanted_ref.shape[0], out_ref.shape[1] // 2 - SUB
    rows = held.shape[0] // 2
    held[:rows] = own_ref[:rows].astype(jnp.float32)
    held[rows:] = other_ref[:rows].astype(jnp.float32)

    def at(d, r):
        return held[pl.ds(pl.multiple_of(wanted_ref[d, r], SUB), SUB), :]

    def body(d, carry):
        for block in range(2):
            for r in range(0, cap, 2):
                to = block * lines + r * SUB
                one = at(d, block * cap + r)
                two = at(d, block * cap + r + 1) if r + 1 < cap else jnp.zeros_like(one)
                out_ref[d, to : to + 2 * SUB, :] = jnp.concatenate([one, two], axis=0).astype(jnp.bfloat16)
        return carry

    lax.fori_loop(0, peers, body, 0, unroll=2)

    tx, th, tl = (lax.axis_index(axis) for axis in AXES)
    deep, span = lax.axis_size("tx"), lax.axis_size("tl")
    edges = edges_ref[...].astype(jnp.float32)
    none = jnp.zeros((SUB, LANES), jnp.float32)
    own = jnp.concatenate([none, own_ref[rows:].astype(jnp.float32)[:SUB]], axis=0).astype(jnp.bfloat16)
    other = jnp.concatenate([none, other_ref[rows:].astype(jnp.float32)[:SUB]], axis=0).astype(jnp.bfloat16)
    top = jnp.concatenate([edges[:SUB], none], axis=0).astype(jnp.bfloat16)
    bottom = jnp.concatenate([edges[SUB:], none], axis=0).astype(jnp.bfloat16)
    for there, x, y, block in (
        (tx > 0, tx - 1, tl, top),
        (tx < deep - 1, tx + 1, tl, bottom),
        (tl > 0, tx, tl - 1, own),
        (tl < span - 1, tx, tl + 1, own),
        ((th == 0) & (tl == 0), tx, span - 1, other),
        ((th == 1) & (tl == span - 1), tx, 0, other),
    ):

        @pl.when(there)
        def _(x=x, y=y, block=block):
            out_ref[jnp.clip(x * span + y, 0, peers - 1), 2 * lines :, :] = block


def gather(wanted, own, other, edges, after, lines):
    peers = wanted.shape[0]
    return pl.pallas_call(
        functools.partial(gather_kernel, wanted.shape[1] // 2),
        in_specs=[whole(pltpu.SMEM), whole(), whole(), whole(), whole(pl.ANY)],
        out_specs=whole(),
        out_shape=jax.ShapeDtypeStruct((peers, 2 * lines + 2 * SUB, LANES), jnp.bfloat16),
        scratch_shapes=[pltpu.VMEM((2 * own.shape[0] - 4 * SUB, LANES), jnp.float32)],
        compiler_params=params(8),
        name="gather",
    )(wanted, own, other, edges, after)


def smooth(field_ref, fetched_ref, at, out_ref):
    beacons, rows, cols = field_ref.shape
    tx, th, tl = (lax.axis_index(axis) for axis in AXES)
    deep, span = lax.axis_size("tx"), lax.axis_size("tl")
    peers = fetched_ref.shape[0]

    def edge(there, x, y):
        peer = jnp.clip(x * span + y, 0, peers - 1)
        return jnp.where(there, fetched_ref[peer, at : at + 2 * SUB, :].astype(jnp.float32), 0.0)

    def line_of(block, k):
        return jnp.concatenate([block[2 * k : 2 * k + 1], block[2 * k + 1 : 2 * k + 2]], axis=1)

    above, below = edge(tx > 0, tx - 1, tl), edge(tx < deep - 1, tx + 1, tl)
    left = edge((tl > 0) | (th == 1), tx, jnp.where(tl > 0, tl - 1, span - 1))
    right = edge((tl < span - 1) | (th == 0), tx, jnp.where(tl < span - 1, tl + 1, 0))
    sides = jnp.concatenate([left[SUB : SUB + beacons], right[SUB + beacons : SUB + 2 * beacons]], axis=0).T
    row = lax.broadcasted_iota(jnp.int32, (rows, cols), 0)
    col = lax.broadcasted_iota(jnp.int32, (rows, cols), 1)
    for k in range(beacons):
        x = field_ref[k]
        near = jnp.where(row == 0, line_of(above, k), pltpu.roll(x, 1, 0))
        near += jnp.where(row == rows - 1, line_of(below, k), pltpu.roll(x, rows - 1, 0))
        near += jnp.where(col == 0, sides[:, k : k + 1], pltpu.roll(x, 1, 1))
        near += jnp.where(col == cols - 1, sides[:, beacons + k : beacons + k + 1], pltpu.roll(x, cols - 1, 1))
        out_ref[k] = smooth_weight * (4.0 * x - near)


def bins_kernel(
    group, line_ref, fetched_ref, blocks_ref, field_ref, out_ref, smooth_ref, held_ref, turn_a, turn_b, samp_a, samp_b, pick, ret, sems
):
    devices, lines, _ = out_ref.shape
    count, samples, cells = blocks_ref.shape
    groups, pairs = count // group, group // 2

    def fetch(i):
        part = pl.ds(i * group, group)
        return pltpu.make_async_copy(blocks_ref.at[part], held_ref.at[part], sems.at[i])

    for i in range(groups):
        fetch(i).start()
    for d in range(devices):
        pick[pl.ds(d * lines, lines), :] = fetched_ref[d // 2, d % 2 * lines : (d % 2 + 1) * lines, :].astype(jnp.float32)
        ret[pl.ds(d * lines, lines), :] = jnp.zeros((lines, LANES), jnp.float32)
    samp_b[...] = jnp.zeros_like(samp_b)
    smooth(field_ref, fetched_ref, 2 * lines, smooth_ref)
    low = lax.broadcasted_iota(jnp.int32, (SUB, LANES), 0) < 4

    def weights(g, p):
        return held_ref[pl.ds(g * group + 2 * p, 2)].reshape(2 * samples, cells)

    def turn(g, to):
        for p in range(pairs):
            to[p] = weights(g, p).T

    def line(b, back):
        return pl.ds(pl.multiple_of(line_ref[back, b], SUB), SUB)

    def sample(g, turned, to):
        for p in range(pairs):
            f0 = pick[line(g * group + 2 * p, 0), :]
            f1 = pick[line(g * group + 2 * p + 1, 0), :]
            left = jnp.where(low, f0, pltpu.roll(f1, 4, 0))
            right = jnp.where(low, pltpu.roll(f0, 4, 0), f1)
            x = jnp.concatenate([left, right], axis=1).astype(jnp.bfloat16)
            s = jnp.dot(x, turned[p], preferred_element_type=jnp.float32)
            to[p] = jnp.concatenate([jnp.where(low, s[:, :samples], 0.0), jnp.where(low, 0.0, s[:, samples:])], axis=1)

    def spread(g, sampled):
        for p in range(pairs):
            a = jnp.dot(sampled[p].astype(jnp.bfloat16), weights(g, p), preferred_element_type=jnp.float32)
            left, right = a[:, :LANES], a[:, LANES:]
            ret[line(g * group + 2 * p, 1), :] = jnp.where(low, left, pltpu.roll(right, 4, 0))
            ret[line(g * group + 2 * p + 1, 1), :] = jnp.where(low, pltpu.roll(left, 4, 0), right)

    fetch(0).wait()
    turn(0, turn_a)

    def body(i, carry):
        g = 2 * i
        fetch(g + 1).wait()

        @pl.when(g + 2 < groups)
        def _():
            fetch(g + 2).wait()

        turn(g + 1, turn_b)
        sample(g, turn_a, samp_a)
        spread(jnp.maximum(g - 1, 0), samp_b)
        turn(jnp.minimum(g + 2, groups - 1), turn_a)
        sample(g + 1, turn_b, samp_b)
        spread(g, samp_a)
        return carry

    lax.fori_loop(0, groups // 2, body, 0)
    spread(groups - 1, samp_b)
    for d in range(devices):
        out_ref[d] = ret[pl.ds(d * lines, lines), :].astype(jnp.bfloat16)


def bins(line, fetched, blocks, field, lines):
    count, samples, cells = blocks.shape
    devices = 2 * fetched.shape[0]
    group = 16
    return pl.pallas_call(
        functools.partial(bins_kernel, group),
        in_specs=[whole(pltpu.SMEM), whole(), whole(pl.ANY), whole()],
        out_specs=[whole()] * 2,
        out_shape=[
            jax.ShapeDtypeStruct((devices, lines, LANES), jnp.bfloat16),
            jax.ShapeDtypeStruct(field.shape, jnp.float32),
        ],
        scratch_shapes=[pltpu.VMEM(blocks.shape, jnp.bfloat16)]
        + [pltpu.VMEM((group // 2, cells, 2 * samples), jnp.bfloat16)] * 2
        + [pltpu.VMEM((group // 2, SUB, 2 * samples), jnp.float32)] * 2
        + [pltpu.VMEM((devices * lines, LANES), jnp.float32)] * 2
        + [pltpu.SemaphoreType.DMA((count // group,))],
        compiler_params=params(50),
        name="bins",
    )(line, fetched, blocks, field)


def image_kernel(near_ref, far_ref, arrived_ref, smooth_ref, direction_ref, residual_ref, image_ref, stats_ref, *sums):
    peers, cap = near_ref.shape[0], near_ref.shape[1] // 2
    beacons, rows, cols = direction_ref.shape
    bands, groups = rows // TILE_SIDE, cols // LANES
    span = lax.axis_size("tl")
    half = lax.axis_index("th")
    for total in sums:
        total[...] = jnp.zeros_like(total)

    def body(q, carry):
        row, place = lax.div(q, span) * (2 * span), lax.rem(q, span)
        for away in range(2):
            d = row + (1 - half if away else half) * span + place
            for r in range(0, cap, 2):
                pair = arrived_ref[d, r * SUB : (r + 2) * SUB, :].astype(jnp.float32)
                for e in range(min(2, cap - r)):
                    first = far_ref[q, cap + r + e] - sums[0].shape[0] if away else near_ref[q, r + e]
                    if away:
                        first = jnp.maximum(first, 0)
                    at = pl.ds(pl.multiple_of(first, SUB), SUB)
                    sums[(r + e) % len(sums)][at, :] += pair[e * SUB : (e + 1) * SUB]
        return carry

    lax.fori_loop(0, peers, body, 0)
    lines = []
    units = []
    for k in range(beacons):
        unit = jnp.zeros((SUB, LANES), jnp.float32)
        for g in range(groups):
            x = []
            for band in range(bands):
                for h in range(2):
                    at = pl.ds((band * groups + g) * SUB * SUB + h * beacons + k, SUB, stride=SUB)
                    x.append(sum(total[at, :] for total in sums))
            x = jnp.concatenate(swap_chunks(x), axis=0)
            x = x + smooth_ref[k, :, g * LANES : (g + 1) * LANES]
            image_ref[k, :, g * LANES : (g + 1) * LANES] = x
            unit = jnp.maximum(unit, jnp.max(jnp.abs(x).reshape(bands * 2, SUB, LANES), axis=0))
        unit = jnp.maximum(unit, 1e-30)
        inverse = 1.0 / unit
        terms = [jnp.zeros((SUB, LANES), jnp.float32)] * 4
        for i in range(rows // SUB):
            for g in range(groups):
                at = (k, slice(i * SUB, (i + 1) * SUB), slice(g * LANES, (g + 1) * LANES))
                x, d, r = image_ref[at], direction_ref[at], residual_ref[at]
                scaled = x * inverse
                terms = [t + v for t, v in zip(terms, (r * r, d * x, r * scaled, scaled * scaled))]
        lines.append(terms)
        units.append(unit)
    largest = [jnp.max(unit, axis=(0, 1), keepdims=True) for unit in units]
    rows_of = []
    for q in range(4):
        for k in range(beacons):
            t = lines[k][q]
            if q >= 2:
                share = units[k] * (1.0 / largest[k])
                t = t * share if q == 2 else t * share * share
            rows_of.append(jnp.sum(t, axis=0, keepdims=True))
    for k in range(beacons):
        first = lax.broadcasted_iota(jnp.int32, (1, LANES), 1) == 0
        rows_of.append(jnp.where(first, largest[k], 0.0))
    rows_of.append(jnp.zeros((LANES - len(rows_of), LANES), jnp.float32))
    stats = jnp.sum(jnp.concatenate(rows_of, axis=0).T, axis=0, keepdims=True)
    stats_ref[...] = jnp.broadcast_to(stats, stats_ref.shape)


def image_of(near, far, arrived, smooth, direction, residual):
    beacons, rows, cols = direction.shape
    return pl.pallas_call(
        image_kernel,
        in_specs=[whole(pltpu.SMEM)] * 2 + [whole()] * 4,
        out_specs=[whole(), whole()],
        out_shape=[
            jax.ShapeDtypeStruct(direction.shape, jnp.float32),
            jax.ShapeDtypeStruct((arrived.shape[0], LANES), jnp.float32),
        ],
        scratch_shapes=[pltpu.VMEM((beacons * rows * cols // LANES, LANES), jnp.float32)] * 4,
        compiler_params=params(16),
        name="image",
    )(near, far, arrived, smooth, direction, residual)


def update_kernel(
    stats_ref, solution_ref, residual_ref, direction_ref, image_ref, sol_ref, res_ref, dir_ref, sol, res, dire, sems
):
    beacons = direction_ref.shape[0]
    stats = stats_ref[...]

    def column(x, q):
        return pltpu.roll(x, LANES - q * beacons, 1) if q else x

    total = jnp.sum(stats, axis=0, keepdims=True)
    total = jnp.broadcast_to(total, (SUB, LANES))
    alpha = total / column(total, 1)
    size = alpha[:1] * column(stats, 4)
    moved = jnp.sum(size * (size * column(stats, 3) - 2.0 * column(stats, 2)), axis=0, keepdims=True)
    beta = (total + moved) / total
    copies = []
    for k in range(beacons):
        a, b = alpha[:1, k : k + 1], beta[:1, k : k + 1]
        d = direction_ref[k]
        r = residual_ref[k] - a * image_ref[k]
        sol[k] = solution_ref[k] + a * d
        res[k] = r
        dire[k] = r + b * d
        for q, (held, out) in enumerate(((sol, sol_ref), (res, res_ref), (dire, dir_ref))):
            copies.append(pltpu.make_async_copy(held.at[k], out.at[k], sems.at[q, k]))
            copies[-1].start()
    for copy in copies:
        copy.wait()


def update(stats, solution, residual, direction, image):
    return pl.pallas_call(
        update_kernel,
        in_specs=[whole()] * 5,
        out_specs=[whole(pl.ANY)] * 3,
        out_shape=[jax.ShapeDtypeStruct(direction.shape, jnp.float32)] * 3,
        scratch_shapes=[pltpu.VMEM(direction.shape, jnp.float32)] * 3
        + [pltpu.SemaphoreType.DMA((3, direction.shape[0]))],
        compiler_params=params(16),
        name="update",
    )(stats, solution, residual, direction, image)


def exchange(x, axes):
    return lax.all_to_all(x, axes, split_axis=0, concat_axis=0, tiled=True)


def trade(x):
    return lax.ppermute(x, "th", [(0, 1), (1, 0)])


def per_device(solution, residual, direction, blocks, bin_owner, bin_tile):
    devices, span = lax.axis_size(AXES), lax.axis_size("tl")
    count = blocks.shape[0]
    cap = max(2, 3 * count // (2 * devices))
    lines = -(-cap // 2) * 2 * SUB
    beacons, rows, cols = direction.shape

    own, edges, direction = tiles(direction)
    other = trade(own)
    both = jnp.concatenate([bin_owner.reshape(1, count), bin_tile.reshape(1, count)], axis=0)
    line, request = prep(both, devices, cap, lines, span, rows * cols // TILE_SIDE**2)
    near = exchange(request.reshape(devices // 2, 2 * cap), HALF)
    far = trade(near)
    fetched = exchange(gather(near, own, other, edges, far, lines), HALF)
    returned, smoothed = bins(line, fetched, blocks, direction, lines)
    arrived = exchange(returned, AXES)
    image, stats = image_of(near, far, arrived, smoothed, direction, residual)
    return update(exchange(stats, AXES), solution, residual, direction, image)


def solution(mesh):
    rows, cols = mesh.devices.shape
    halves = jax.sharding.Mesh(mesh.devices.reshape(rows, 2, cols // 2), AXES)
    field = P(None, "tx", TY)
    return jax.shard_map(
        per_device,
        mesh=halves,
        in_specs=(field, field, field, P(AXES, None, None), P(AXES, None), P(AXES)),
        out_specs=(field,) * 3,
        check_vma=False,
    )
```

```python
import functools

import jax
import jax.numpy as jnp
from jax import lax
from jax.experimental import pallas as pl
from jax.experimental.pallas import tpu as pltpu
from jax.sharding import PartitionSpec as P

TILE_SIDE = 16
LANES = 128
SUB = 8
smooth_weight = 0.25

TY = ("th", "tl")
AXES = ("tx", "th", "tl")
HALF = ("tx", "tl")


def whole(memory=pltpu.VMEM):
    return pl.BlockSpec(memory_space=memory)


def params(mib):
    return pltpu.CompilerParams(vmem_limit_bytes=mib << 20)


def swap_chunks(blocks):
    row = lax.broadcasted_iota(jnp.int32, (SUB, LANES), 0)
    lane = lax.broadcasted_iota(jnp.int32, (SUB, LANES), 1)
    chunk, rest = lane // TILE_SIDE, lane % TILE_SIDE
    first = (chunk + row) % SUB * TILE_SIDE + rest
    second = (row - chunk + SUB) % SUB * TILE_SIDE + rest

    def swap(x):
        x = jnp.take_along_axis(x, first, axis=1)
        for s in (1, 2, 4):
            x = jnp.where((chunk & s) != 0, pltpu.roll(x, s, 0), x)
        return jnp.take_along_axis(x, second, axis=1)

    return [swap(x) for x in blocks]


def prep_kernel(step, span, tiles, both_ref, line_ref, request_ref):
    devices, bins = request_ref.shape[0], both_ref.shape[1]
    owner, tile = both_ref[:1], both_ref[1:]
    column = lax.rem(owner, 2 * span)
    far = (lax.div(column, span) != lax.axis_index("th")).astype(jnp.int32)
    place = (lax.div(owner, 2 * span) * span + lax.rem(column, span)) * 2 + far
    earlier = (
        lax.broadcasted_iota(jnp.int32, (bins, bins), 0) < lax.broadcasted_iota(jnp.int32, (bins, bins), 1)
    ).astype(jnp.bfloat16)
    member = (lax.broadcasted_iota(jnp.int32, (devices, bins), 0) == place).astype(jnp.float32)
    member16 = member.astype(jnp.bfloat16)
    before = jnp.dot(member16, earlier, preferred_element_type=jnp.float32)
    rank = jnp.sum(before * member, axis=0, keepdims=True).astype(jnp.int32)
    line_ref[:1] = place * step + rank * SUB
    line_ref[1:] = owner * step + rank * SUB
    at = lax.broadcasted_iota(jnp.int32, (request_ref.shape[1], bins), 0) == rank
    named = jnp.where(at, tile + far * tiles, 0).astype(jnp.float32).astype(jnp.bfloat16)
    request = lax.dot_general(member16, named, (((1,), (1,)), ((), ())), preferred_element_type=jnp.float32)
    request_ref[...] = request.astype(jnp.int32) * SUB


def prep(both, devices, cap, lines, span, tiles):
    bins = both.shape[1]
    return pl.pallas_call(
        functools.partial(prep_kernel, lines, span, tiles),
        in_specs=[whole()],
        out_specs=[whole()] * 2,
        out_shape=[
            jax.ShapeDtypeStruct((2, bins), jnp.int32),
            jax.ShapeDtypeStruct((devices, cap), jnp.int32),
        ],
        compiler_params=params(4),
        name="prep",
    )(both)


def tiles_kernel(field_ref, out_ref, edges_ref, copy_ref, held):
    beacons, rows, cols = field_ref.shape
    bands, groups = rows // TILE_SIDE, cols // LANES
    for k in range(beacons):
        for g in range(groups):
            x = field_ref[k, :, g * LANES : (g + 1) * LANES]
            x = swap_chunks([x[i * SUB : (i + 1) * SUB] for i in range(bands * 2)])
            for band in range(bands):
                for h in range(2):
                    at = (band * groups + g) * SUB * SUB + h * beacons + k
                    held[pl.ds(at, SUB, stride=SUB), :] = x[band * 2 + h]
    copy_ref[...] = field_ref[...]
    count = held.shape[0]
    out_ref[:count] = held[...].astype(jnp.bfloat16)
    ends = [field_ref[k, r : r + 1, g * LANES : (g + 1) * LANES] for r in (0, rows - 1) for k in range(beacons) for g in range(groups)]
    edges_ref[...] = jnp.concatenate(ends, axis=0).astype(jnp.bfloat16)
    lane = lax.broadcasted_iota(jnp.int32, (rows, LANES), 1)
    sides = jnp.zeros((rows, LANES), jnp.float32)
    for k in range(beacons):
        sides = jnp.where(lane == k, field_ref[k, :, cols - 1 :], sides)
        sides = jnp.where(lane == beacons + k, field_ref[k, :, :1], sides)
    out_ref[count:] = sides.T[: 2 * SUB].astype(jnp.bfloat16)


def tiles(field):
    beacons, rows, cols = field.shape
    return pl.pallas_call(
        tiles_kernel,
        in_specs=[whole()],
        out_specs=[whole()] * 3,
        out_shape=[
            jax.ShapeDtypeStruct((beacons * rows * cols // LANES + 2 * SUB, LANES), jnp.bfloat16),
            jax.ShapeDtypeStruct((2 * SUB, LANES), jnp.bfloat16),
            jax.ShapeDtypeStruct(field.shape, field.dtype),
        ],
        scratch_shapes=[pltpu.VMEM((beacons * rows * cols // LANES, LANES), jnp.float32)],
        compiler_params=params(8),
        name="tiles",
    )(field)


def gather_kernel(cap, wanted_vmem, own_ref, other_ref, edges_ref, after_ref, out_ref, held, wanted_ref, sem):
    copy = pltpu.make_async_copy(wanted_vmem, wanted_ref, sem)
    copy.start()
    peers, lines = wanted_ref.shape[0], out_ref.shape[1] // 2 - SUB
    rows = held.shape[0] // 2
    held[:rows] = own_ref[:rows].astype(jnp.float32)
    held[rows:] = other_ref[:rows].astype(jnp.float32)
    copy.wait()

    def at(d, r):
        return held[pl.ds(pl.multiple_of(wanted_ref[d, r], SUB), SUB), :]

    def body(d, carry):
        for block in range(2):
            for r in range(0, cap, 2):
                to = block * lines + r * SUB
                one = at(d, block * cap + r)
                two = at(d, block * cap + r + 1) if r + 1 < cap else jnp.zeros_like(one)
                out_ref[d, to : to + 2 * SUB, :] = jnp.concatenate([one, two], axis=0).astype(jnp.bfloat16)
        return carry

    lax.fori_loop(0, peers, body, 0, unroll=2)

    tx, th, tl = (lax.axis_index(axis) for axis in AXES)
    deep, span = lax.axis_size("tx"), lax.axis_size("tl")
    edges = edges_ref[...].astype(jnp.float32)
    none = jnp.zeros((SUB, LANES), jnp.float32)
    own = jnp.concatenate([none, own_ref[rows:].astype(jnp.float32)[:SUB]], axis=0).astype(jnp.bfloat16)
    other = jnp.concatenate([none, other_ref[rows:].astype(jnp.float32)[:SUB]], axis=0).astype(jnp.bfloat16)
    top = jnp.concatenate([edges[:SUB], none], axis=0).astype(jnp.bfloat16)
    bottom = jnp.concatenate([edges[SUB:], none], axis=0).astype(jnp.bfloat16)
    for there, x, y, block in (
        (tx > 0, tx - 1, tl, top),
        (tx < deep - 1, tx + 1, tl, bottom),
        (tl > 0, tx, tl - 1, own),
        (tl < span - 1, tx, tl + 1, own),
        ((th == 0) & (tl == 0), tx, span - 1, other),
        ((th == 1) & (tl == span - 1), tx, 0, other),
    ):

        @pl.when(there)
        def _(x=x, y=y, block=block):
            out_ref[jnp.clip(x * span + y, 0, peers - 1), 2 * lines :, :] = block


def gather(wanted, own, other, edges, after, lines):
    peers = wanted.shape[0]
    return pl.pallas_call(
        functools.partial(gather_kernel, wanted.shape[1] // 2),
        in_specs=[whole()] * 4 + [whole(pl.ANY)],
        out_specs=whole(),
        out_shape=jax.ShapeDtypeStruct((peers, 2 * lines + 2 * SUB, LANES), jnp.bfloat16),
        scratch_shapes=[
            pltpu.VMEM((2 * own.shape[0] - 4 * SUB, LANES), jnp.float32),
            pltpu.SMEM(wanted.shape, jnp.int32),
            pltpu.SemaphoreType.DMA,
        ],
        compiler_params=params(8),
        name="gather",
    )(wanted, own, other, edges, after)


def smooth(field_ref, fetched_ref, at, out_ref):
    beacons, rows, cols = field_ref.shape
    tx, th, tl = (lax.axis_index(axis) for axis in AXES)
    deep, span = lax.axis_size("tx"), lax.axis_size("tl")
    peers = fetched_ref.shape[0]

    def edge(there, x, y):
        peer = jnp.clip(x * span + y, 0, peers - 1)
        return jnp.where(there, fetched_ref[peer, at : at + 2 * SUB, :].astype(jnp.float32), 0.0)

    def line_of(block, k):
        return jnp.concatenate([block[2 * k : 2 * k + 1], block[2 * k + 1 : 2 * k + 2]], axis=1)

    above, below = edge(tx > 0, tx - 1, tl), edge(tx < deep - 1, tx + 1, tl)
    left = edge((tl > 0) | (th == 1), tx, jnp.where(tl > 0, tl - 1, span - 1))
    right = edge((tl < span - 1) | (th == 0), tx, jnp.where(tl < span - 1, tl + 1, 0))
    sides = jnp.concatenate([left[SUB : SUB + beacons], right[SUB + beacons : SUB + 2 * beacons]], axis=0).T
    row = lax.broadcasted_iota(jnp.int32, (rows, cols), 0)
    col = lax.broadcasted_iota(jnp.int32, (rows, cols), 1)
    for k in range(beacons):
        x = field_ref[k]
        near = jnp.where(row == 0, line_of(above, k), pltpu.roll(x, 1, 0))
        near += jnp.where(row == rows - 1, line_of(below, k), pltpu.roll(x, rows - 1, 0))
        near += jnp.where(col == 0, sides[:, k : k + 1], pltpu.roll(x, 1, 1))
        near += jnp.where(col == cols - 1, sides[:, beacons + k : beacons + k + 1], pltpu.roll(x, cols - 1, 1))
        out_ref[k] = smooth_weight * (4.0 * x - near)


def bins_kernel(
    group, line_vmem, fetched_ref, blocks_ref, field_ref, out_ref, smooth_ref, *scratch
):
    held_ref, turn_a, turn_b, samp_a, samp_b, pick, ret, line_ref, sems, sem = scratch
    devices, lines, _ = out_ref.shape
    count, samples, cells = blocks_ref.shape
    groups, pairs = count // group, group // 2

    def fetch(i):
        part = pl.ds(i * group, group)
        return pltpu.make_async_copy(blocks_ref.at[part], held_ref.at[part], sems.at[i])

    for i in range(groups):
        fetch(i).start()
    copy = pltpu.make_async_copy(line_vmem, line_ref, sem)
    copy.start()
    for d in range(devices):
        pick[pl.ds(d * lines, lines), :] = fetched_ref[d // 2, d % 2 * lines : (d % 2 + 1) * lines, :].astype(jnp.float32)
        ret[pl.ds(d * lines, lines), :] = jnp.zeros((lines, LANES), jnp.float32)
    samp_b[...] = jnp.zeros_like(samp_b)
    smooth(field_ref, fetched_ref, 2 * lines, smooth_ref)
    low = lax.broadcasted_iota(jnp.int32, (SUB, LANES), 0) < 4

    def weights(g, p):
        return held_ref[pl.ds(g * group + 2 * p, 2)].reshape(2 * samples, cells)

    def turn(g, to):
        for p in range(pairs):
            to[p] = weights(g, p).T

    def line(b, back):
        return pl.ds(pl.multiple_of(line_ref[back, b], SUB), SUB)

    def sample(g, turned, to):
        for p in range(pairs):
            f0 = pick[line(g * group + 2 * p, 0), :]
            f1 = pick[line(g * group + 2 * p + 1, 0), :]
            left = jnp.where(low, f0, pltpu.roll(f1, 4, 0))
            right = jnp.where(low, pltpu.roll(f0, 4, 0), f1)
            x = jnp.concatenate([left, right], axis=1).astype(jnp.bfloat16)
            s = jnp.dot(x, turned[p], preferred_element_type=jnp.float32)
            to[p] = jnp.concatenate([jnp.where(low, s[:, :samples], 0.0), jnp.where(low, 0.0, s[:, samples:])], axis=1)

    def spread(g, sampled):
        for p in range(pairs):
            a = jnp.dot(sampled[p].astype(jnp.bfloat16), weights(g, p), preferred_element_type=jnp.float32)
            left, right = a[:, :LANES], a[:, LANES:]
            ret[line(g * group + 2 * p, 1), :] = jnp.where(low, left, pltpu.roll(right, 4, 0))
            ret[line(g * group + 2 * p + 1, 1), :] = jnp.where(low, pltpu.roll(left, 4, 0), right)

    copy.wait()
    fetch(0).wait()
    turn(0, turn_a)

    def body(i, carry):
        g = 2 * i
        fetch(g + 1).wait()

        @pl.when(g + 2 < groups)
        def _():
            fetch(g + 2).wait()

        turn(g + 1, turn_b)
        sample(g, turn_a, samp_a)
        spread(jnp.maximum(g - 1, 0), samp_b)
        turn(jnp.minimum(g + 2, groups - 1), turn_a)
        sample(g + 1, turn_b, samp_b)
        spread(g, samp_a)
        return carry

    lax.fori_loop(0, groups // 2, body, 0)
    spread(groups - 1, samp_b)
    for d in range(devices):
        out_ref[d] = ret[pl.ds(d * lines, lines), :].astype(jnp.bfloat16)


def bins(line, fetched, blocks, field, lines):
    count, samples, cells = blocks.shape
    devices = 2 * fetched.shape[0]
    group = 16
    return pl.pallas_call(
        functools.partial(bins_kernel, group),
        in_specs=[whole(), whole(), whole(pl.ANY), whole()],
        out_specs=[whole()] * 2,
        out_shape=[
            jax.ShapeDtypeStruct((devices, lines, LANES), jnp.bfloat16),
            jax.ShapeDtypeStruct(field.shape, jnp.float32),
        ],
        scratch_shapes=[pltpu.VMEM(blocks.shape, jnp.bfloat16)]
        + [pltpu.VMEM((group // 2, cells, 2 * samples), jnp.bfloat16)] * 2
        + [pltpu.VMEM((group // 2, SUB, 2 * samples), jnp.float32)] * 2
        + [pltpu.VMEM((devices * lines, LANES), jnp.float32)] * 2
        + [pltpu.SMEM(line.shape, jnp.int32), pltpu.SemaphoreType.DMA((count // group,)), pltpu.SemaphoreType.DMA],
        compiler_params=params(50),
        name="bins",
    )(line, fetched, blocks, field)


def image_kernel(near_vmem, far_vmem, arrived_ref, smooth_ref, direction_ref, residual_ref, image_ref, stats_ref, *scratch):
    *sums, near_ref, far_ref, sems = scratch
    copies = [
        pltpu.make_async_copy(a, b, sems.at[i]) for i, (a, b) in enumerate(((near_vmem, near_ref), (far_vmem, far_ref)))
    ]
    for copy in copies:
        copy.start()
    peers, cap = near_ref.shape[0], near_ref.shape[1] // 2
    beacons, rows, cols = direction_ref.shape
    bands, groups = rows // TILE_SIDE, cols // LANES
    span = lax.axis_size("tl")
    half = lax.axis_index("th")
    for total in sums:
        total[...] = jnp.zeros_like(total)
    for copy in copies:
        copy.wait()

    def body(q, carry):
        row, place = lax.div(q, span) * (2 * span), lax.rem(q, span)
        for away in range(2):
            d = row + (1 - half if away else half) * span + place
            for r in range(0, cap, 2):
                pair = arrived_ref[d, r * SUB : (r + 2) * SUB, :].astype(jnp.float32)
                for e in range(min(2, cap - r)):
                    first = far_ref[q, cap + r + e] - sums[0].shape[0] if away else near_ref[q, r + e]
                    if away:
                        first = jnp.maximum(first, 0)
                    at = pl.ds(pl.multiple_of(first, SUB), SUB)
                    sums[(r + e) % len(sums)][at, :] += pair[e * SUB : (e + 1) * SUB]
        return carry

    lax.fori_loop(0, peers, body, 0)
    lines = []
    units = []
    for k in range(beacons):
        unit = jnp.zeros((SUB, LANES), jnp.float32)
        for g in range(groups):
            x = []
            for band in range(bands):
                for h in range(2):
                    at = pl.ds((band * groups + g) * SUB * SUB + h * beacons + k, SUB, stride=SUB)
                    x.append(sum(total[at, :] for total in sums))
            x = jnp.concatenate(swap_chunks(x), axis=0)
            x = x + smooth_ref[k, :, g * LANES : (g + 1) * LANES]
            image_ref[k, :, g * LANES : (g + 1) * LANES] = x
            unit = jnp.maximum(unit, jnp.max(jnp.abs(x).reshape(bands * 2, SUB, LANES), axis=0))
        unit = jnp.maximum(unit, 1e-30)
        inverse = 1.0 / unit
        terms = [jnp.zeros((SUB, LANES), jnp.float32)] * 4
        for i in range(rows // SUB):
            for g in range(groups):
                at = (k, slice(i * SUB, (i + 1) * SUB), slice(g * LANES, (g + 1) * LANES))
                x, d, r = image_ref[at], direction_ref[at], residual_ref[at]
                scaled = x * inverse
                terms = [t + v for t, v in zip(terms, (r * r, d * x, r * scaled, scaled * scaled))]
        lines.append(terms)
        units.append(unit)
    largest = [jnp.max(unit, axis=(0, 1), keepdims=True) for unit in units]
    rows_of = []
    for q in range(4):
        for k in range(beacons):
            t = lines[k][q]
            if q >= 2:
                share = units[k] * (1.0 / largest[k])
                t = t * share if q == 2 else t * share * share
            rows_of.append(jnp.sum(t, axis=0, keepdims=True))
    for k in range(beacons):
        first = lax.broadcasted_iota(jnp.int32, (1, LANES), 1) == 0
        rows_of.append(jnp.where(first, largest[k], 0.0))
    rows_of.append(jnp.zeros((LANES - len(rows_of), LANES), jnp.float32))
    stats = jnp.sum(jnp.concatenate(rows_of, axis=0).T, axis=0, keepdims=True)
    stats_ref[...] = jnp.broadcast_to(stats, stats_ref.shape)


def image_of(near, far, arrived, smooth, direction, residual):
    beacons, rows, cols = direction.shape
    return pl.pallas_call(
        image_kernel,
        in_specs=[whole()] * 6,
        out_specs=[whole(), whole()],
        out_shape=[
            jax.ShapeDtypeStruct(direction.shape, jnp.float32),
            jax.ShapeDtypeStruct((arrived.shape[0], LANES), jnp.float32),
        ],
        scratch_shapes=[pltpu.VMEM((beacons * rows * cols // LANES, LANES), jnp.float32)] * 4
        + [pltpu.SMEM(near.shape, jnp.int32)] * 2
        + [pltpu.SemaphoreType.DMA((2,))],
        compiler_params=params(16),
        name="image",
    )(near, far, arrived, smooth, direction, residual)


def update_kernel(
    stats_ref, solution_ref, residual_ref, direction_ref, image_ref, sol_ref, res_ref, dir_ref, sol, res, dire, sems
):
    beacons = direction_ref.shape[0]
    stats = stats_ref[...]

    def column(x, q):
        return pltpu.roll(x, LANES - q * beacons, 1) if q else x

    total = jnp.sum(stats, axis=0, keepdims=True)
    total = jnp.broadcast_to(total, (SUB, LANES))
    alpha = total / column(total, 1)
    size = alpha[:1] * column(stats, 4)
    moved = jnp.sum(size * (size * column(stats, 3) - 2.0 * column(stats, 2)), axis=0, keepdims=True)
    beta = (total + moved) / total
    copies = []
    for k in range(beacons):
        a, b = alpha[:1, k : k + 1], beta[:1, k : k + 1]
        d = direction_ref[k]
        r = residual_ref[k] - a * image_ref[k]
        sol[k] = solution_ref[k] + a * d
        res[k] = r
        dire[k] = r + b * d
        for q, (held, out) in enumerate(((sol, sol_ref), (res, res_ref), (dire, dir_ref))):
            copies.append(pltpu.make_async_copy(held.at[k], out.at[k], sems.at[q, k]))
            copies[-1].start()
    for copy in copies:
        copy.wait()


def update(stats, solution, residual, direction, image):
    return pl.pallas_call(
        update_kernel,
        in_specs=[whole()] * 5,
        out_specs=[whole(pl.ANY)] * 3,
        out_shape=[jax.ShapeDtypeStruct(direction.shape, jnp.float32)] * 3,
        scratch_shapes=[pltpu.VMEM(direction.shape, jnp.float32)] * 3
        + [pltpu.SemaphoreType.DMA((3, direction.shape[0]))],
        compiler_params=params(16),
        name="update",
    )(stats, solution, residual, direction, image)


def exchange(x, axes):
    return lax.all_to_all(x, axes, split_axis=0, concat_axis=0, tiled=True)


def trade(x):
    return lax.ppermute(x, "th", [(0, 1), (1, 0)])


def per_device(solution, residual, direction, blocks, bin_owner, bin_tile):
    devices, span = lax.axis_size(AXES), lax.axis_size("tl")
    count = blocks.shape[0]
    cap = max(2, 3 * count // (2 * devices))
    lines = -(-cap // 2) * 2 * SUB
    beacons, rows, cols = direction.shape

    own, edges, direction = tiles(direction)
    other = trade(own)
    both = jnp.concatenate([bin_owner.reshape(1, count), bin_tile.reshape(1, count)], axis=0)
    line, request = prep(both, devices, cap, lines, span, rows * cols // TILE_SIDE**2)
    near = exchange(request.reshape(devices // 2, 2 * cap), HALF)
    far = trade(near)
    fetched = exchange(gather(near, own, other, edges, far, lines), HALF)
    returned, smoothed = bins(line, fetched, blocks, direction, lines)
    arrived = exchange(returned, AXES)
    image, stats = image_of(near, far, arrived, smoothed, direction, residual)
    return update(exchange(stats, AXES), solution, residual, direction, image)


def solution(mesh):
    rows, cols = mesh.devices.shape
    halves = jax.sharding.Mesh(mesh.devices.reshape(rows, 2, cols // 2), AXES)
    field = P(None, "tx", TY)
    return jax.shard_map(
        per_device,
        mesh=halves,
        in_specs=(field, field, field, P(AXES, None, None), P(AXES, None), P(AXES)),
        out_specs=(field,) * 3,
        check_vma=False,
    )
```

```python
import functools

import jax
import jax.numpy as jnp
from jax import lax
from jax.experimental import pallas as pl
from jax.experimental.pallas import tpu as pltpu
from jax.sharding import PartitionSpec as P

TILE_SIDE = 16
LANES = 128
SUB = 8
smooth_weight = 0.25

TY = ("th", "tl")
AXES = ("tx", "th", "tl")
HALF = ("tx", "tl")


def whole(memory=pltpu.VMEM):
    return pl.BlockSpec(memory_space=memory)


def params(mib):
    return pltpu.CompilerParams(vmem_limit_bytes=mib << 20)


def swap_chunks(blocks):
    row = lax.broadcasted_iota(jnp.int32, (SUB, LANES), 0)
    lane = lax.broadcasted_iota(jnp.int32, (SUB, LANES), 1)
    chunk, rest = lane // TILE_SIDE, lane % TILE_SIDE
    first = (chunk + row) % SUB * TILE_SIDE + rest
    second = (row - chunk + SUB) % SUB * TILE_SIDE + rest

    def swap(x):
        x = jnp.take_along_axis(x, first, axis=1)
        for s in (1, 2, 4):
            x = jnp.where((chunk & s) != 0, pltpu.roll(x, s, 0), x)
        return jnp.take_along_axis(x, second, axis=1)

    return [swap(x) for x in blocks]


def prep_kernel(step, span, tiles, both_ref, line_ref, request_ref):
    devices, bins = request_ref.shape[0], both_ref.shape[1]
    owner, tile = both_ref[:1], both_ref[1:]
    column = lax.rem(owner, 2 * span)
    far = (lax.div(column, span) != lax.axis_index("th")).astype(jnp.int32)
    place = (lax.div(owner, 2 * span) * span + lax.rem(column, span)) * 2 + far
    earlier = (
        lax.broadcasted_iota(jnp.int32, (bins, bins), 0) < lax.broadcasted_iota(jnp.int32, (bins, bins), 1)
    ).astype(jnp.bfloat16)
    member = (lax.broadcasted_iota(jnp.int32, (devices, bins), 0) == place).astype(jnp.float32)
    member16 = member.astype(jnp.bfloat16)
    before = jnp.dot(member16, earlier, preferred_element_type=jnp.float32)
    rank = jnp.sum(before * member, axis=0, keepdims=True).astype(jnp.int32)
    line_ref[:1] = place * step + rank * SUB
    line_ref[1:] = owner * step + rank * SUB
    at = lax.broadcasted_iota(jnp.int32, (request_ref.shape[1], bins), 0) == rank
    named = jnp.where(at, tile + far * tiles, 0).astype(jnp.float32).astype(jnp.bfloat16)
    request = lax.dot_general(member16, named, (((1,), (1,)), ((), ())), preferred_element_type=jnp.float32)
    request_ref[...] = request.astype(jnp.int32) * SUB


def prep(both, devices, cap, lines, span, tiles):
    bins = both.shape[1]
    return pl.pallas_call(
        functools.partial(prep_kernel, lines, span, tiles),
        in_specs=[whole()],
        out_specs=[whole()] * 2,
        out_shape=[
            jax.ShapeDtypeStruct((2, bins), jnp.int32),
            jax.ShapeDtypeStruct((devices, cap), jnp.int32),
        ],
        compiler_params=params(4),
        name="prep",
    )(both)


def tiles_kernel(field_ref, out_ref, edges_ref, copy_ref, held):
    beacons, rows, cols = field_ref.shape
    bands, groups = rows // TILE_SIDE, cols // LANES
    for k in range(beacons):
        for g in range(groups):
            x = field_ref[k, :, g * LANES : (g + 1) * LANES]
            x = swap_chunks([x[i * SUB : (i + 1) * SUB] for i in range(bands * 2)])
            for band in range(bands):
                for h in range(2):
                    at = (band * groups + g) * SUB * SUB + h * beacons + k
                    held[pl.ds(at, SUB, stride=SUB), :] = x[band * 2 + h]
    copy_ref[...] = field_ref[...]
    count = held.shape[0]
    out_ref[:count] = held[...].astype(jnp.bfloat16)
    ends = [field_ref[k, r : r + 1, g * LANES : (g + 1) * LANES] for r in (0, rows - 1) for k in range(beacons) for g in range(groups)]
    edges_ref[...] = jnp.concatenate(ends, axis=0).astype(jnp.bfloat16)
    lane = lax.broadcasted_iota(jnp.int32, (rows, LANES), 1)
    sides = jnp.zeros((rows, LANES), jnp.float32)
    for k in range(beacons):
        sides = jnp.where(lane == k, field_ref[k, :, cols - 1 :], sides)
        sides = jnp.where(lane == beacons + k, field_ref[k, :, :1], sides)
    out_ref[count:] = sides.T[: 2 * SUB].astype(jnp.bfloat16)


def tiles(field):
    beacons, rows, cols = field.shape
    return pl.pallas_call(
        tiles_kernel,
        in_specs=[whole()],
        out_specs=[whole()] * 3,
        out_shape=[
            jax.ShapeDtypeStruct((beacons * rows * cols // LANES + 2 * SUB, LANES), jnp.bfloat16),
            jax.ShapeDtypeStruct((2 * SUB, LANES), jnp.bfloat16),
            jax.ShapeDtypeStruct(field.shape, field.dtype),
        ],
        scratch_shapes=[pltpu.VMEM((beacons * rows * cols // LANES, LANES), jnp.float32)],
        compiler_params=params(8),
        name="tiles",
    )(field)


def gather_kernel(cap, wanted_vmem, own_ref, other_ref, edges_ref, after_ref, out_ref, held, wanted_ref, sem):
    copy = pltpu.make_async_copy(wanted_vmem, wanted_ref, sem)
    copy.start()
    peers, lines = wanted_ref.shape[0], out_ref.shape[1] // 2 - SUB
    rows = held.shape[0] // 2
    held[:rows] = own_ref[:rows].astype(jnp.float32)
    held[rows:] = other_ref[:rows].astype(jnp.float32)
    copy.wait()

    def at(d, r):
        return held[pl.ds(pl.multiple_of(wanted_ref[d, r], SUB), SUB), :]

    def body(d, carry):
        for block in range(2):
            for r in range(0, cap, 2):
                to = block * lines + r * SUB
                one = at(d, block * cap + r)
                two = at(d, block * cap + r + 1) if r + 1 < cap else jnp.zeros_like(one)
                out_ref[d, to : to + 2 * SUB, :] = jnp.concatenate([one, two], axis=0).astype(jnp.bfloat16)
        return carry

    lax.fori_loop(0, peers, body, 0, unroll=2)

    tx, th, tl = (lax.axis_index(axis) for axis in AXES)
    deep, span = lax.axis_size("tx"), lax.axis_size("tl")
    edges = edges_ref[...].astype(jnp.float32)
    none = jnp.zeros((SUB, LANES), jnp.float32)
    own = jnp.concatenate([none, own_ref[rows:].astype(jnp.float32)[:SUB]], axis=0).astype(jnp.bfloat16)
    other = jnp.concatenate([none, other_ref[rows:].astype(jnp.float32)[:SUB]], axis=0).astype(jnp.bfloat16)
    top = jnp.concatenate([edges[:SUB], none], axis=0).astype(jnp.bfloat16)
    bottom = jnp.concatenate([edges[SUB:], none], axis=0).astype(jnp.bfloat16)
    for there, x, y, block in (
        (tx > 0, tx - 1, tl, top),
        (tx < deep - 1, tx + 1, tl, bottom),
        (tl > 0, tx, tl - 1, own),
        (tl < span - 1, tx, tl + 1, own),
        ((th == 0) & (tl == 0), tx, span - 1, other),
        ((th == 1) & (tl == span - 1), tx, 0, other),
    ):

        @pl.when(there)
        def _(x=x, y=y, block=block):
            out_ref[jnp.clip(x * span + y, 0, peers - 1), 2 * lines :, :] = block


def gather(wanted, own, other, edges, after, lines):
    peers = wanted.shape[0]
    return pl.pallas_call(
        functools.partial(gather_kernel, wanted.shape[1] // 2),
        in_specs=[whole()] * 4 + [whole(pl.ANY)],
        out_specs=whole(),
        out_shape=jax.ShapeDtypeStruct((peers, 2 * lines + 2 * SUB, LANES), jnp.bfloat16),
        scratch_shapes=[
            pltpu.VMEM((2 * own.shape[0] - 4 * SUB, LANES), jnp.float32),
            pltpu.SMEM(wanted.shape, jnp.int32),
            pltpu.SemaphoreType.DMA,
        ],
        compiler_params=params(8),
        name="gather",
    )(wanted, own, other, edges, after)


def smooth(field_ref, fetched_ref, at, out_ref):
    beacons, rows, cols = field_ref.shape
    tx, th, tl = (lax.axis_index(axis) for axis in AXES)
    deep, span = lax.axis_size("tx"), lax.axis_size("tl")
    peers = fetched_ref.shape[0]

    def edge(there, x, y):
        peer = jnp.clip(x * span + y, 0, peers - 1)
        return jnp.where(there, fetched_ref[peer, at : at + 2 * SUB, :].astype(jnp.float32), 0.0)

    def line_of(block, k):
        return jnp.concatenate([block[2 * k : 2 * k + 1], block[2 * k + 1 : 2 * k + 2]], axis=1)

    above, below = edge(tx > 0, tx - 1, tl), edge(tx < deep - 1, tx + 1, tl)
    left = edge((tl > 0) | (th == 1), tx, jnp.where(tl > 0, tl - 1, span - 1))
    right = edge((tl < span - 1) | (th == 0), tx, jnp.where(tl < span - 1, tl + 1, 0))
    sides = jnp.concatenate([left[SUB : SUB + beacons], right[SUB + beacons : SUB + 2 * beacons]], axis=0).T
    row = lax.broadcasted_iota(jnp.int32, (rows, cols), 0)
    col = lax.broadcasted_iota(jnp.int32, (rows, cols), 1)
    for k in range(beacons):
        x = field_ref[k]
        near = jnp.where(row == 0, line_of(above, k), pltpu.roll(x, 1, 0))
        near += jnp.where(row == rows - 1, line_of(below, k), pltpu.roll(x, rows - 1, 0))
        near += jnp.where(col == 0, sides[:, k : k + 1], pltpu.roll(x, 1, 1))
        near += jnp.where(col == cols - 1, sides[:, beacons + k : beacons + k + 1], pltpu.roll(x, cols - 1, 1))
        out_ref[k] = smooth_weight * (4.0 * x - near)


def bins_kernel(
    group, line_vmem, fetched_ref, blocks_ref, field_ref, out_ref, smooth_ref, *scratch
):
    held_ref, turn_a, turn_b, samp_a, samp_b, pick, ret, line_ref, sems, sem = scratch
    devices, lines, _ = out_ref.shape
    count, samples, cells = blocks_ref.shape
    groups, pairs = count // group, group // 2

    def fetch(i):
        part = pl.ds(i * group, group)
        return pltpu.make_async_copy(blocks_ref.at[part], held_ref.at[part], sems.at[i])

    for i in range(groups):
        fetch(i).start()
    copy = pltpu.make_async_copy(line_vmem, line_ref, sem)
    copy.start()
    for d in range(devices):
        pick[pl.ds(d * lines, lines), :] = fetched_ref[d // 2, d % 2 * lines : (d % 2 + 1) * lines, :].astype(jnp.float32)
        ret[pl.ds(d * lines, lines), :] = jnp.zeros((lines, LANES), jnp.float32)
    smooth(field_ref, fetched_ref, 2 * lines, smooth_ref)
    low = lax.broadcasted_iota(jnp.int32, (SUB, LANES), 0) < 4

    def weights(g, p):
        return held_ref[pl.ds(g * group + 2 * p, 2)].reshape(2 * samples, cells)

    def turn(g, to):
        for p in range(pairs):
            to[p] = weights(g, p).T

    def line(b, back):
        return pl.ds(pl.multiple_of(line_ref[back, b], SUB), SUB)

    def sample(g, turned, to):
        for p in range(pairs):
            f0 = pick[line(g * group + 2 * p, 0), :]
            f1 = pick[line(g * group + 2 * p + 1, 0), :]
            left = jnp.where(low, f0, pltpu.roll(f1, 4, 0))
            right = jnp.where(low, pltpu.roll(f0, 4, 0), f1)
            x = jnp.concatenate([left, right], axis=1).astype(jnp.bfloat16)
            s = jnp.dot(x, turned[p], preferred_element_type=jnp.float32)
            to[p] = jnp.concatenate([jnp.where(low, s[:, :samples], 0.0), jnp.where(low, 0.0, s[:, samples:])], axis=1)

    def spread(g, sampled):
        for p in range(pairs):
            a = jnp.dot(sampled[p].astype(jnp.bfloat16), weights(g, p), preferred_element_type=jnp.float32)
            left, right = a[:, :LANES], a[:, LANES:]
            ret[line(g * group + 2 * p, 1), :] = jnp.where(low, left, pltpu.roll(right, 4, 0))
            ret[line(g * group + 2 * p + 1, 1), :] = jnp.where(low, pltpu.roll(left, 4, 0), right)

    copy.wait()
    fetch(0).wait()
    turn(0, turn_a)
    fetch(1).wait()
    turn(1, turn_b)
    sample(0, turn_a, samp_a)
    fetch(2).wait()
    turn(2, turn_a)
    sample(1, turn_b, samp_b)
    spread(0, samp_a)

    def body(i, carry):
        g = 2 * i
        fetch(g + 1).wait()

        @pl.when(g + 2 < groups)
        def _():
            fetch(g + 2).wait()

        turn(g + 1, turn_b)
        sample(g, turn_a, samp_a)
        spread(g - 1, samp_b)
        turn(jnp.minimum(g + 2, groups - 1), turn_a)
        sample(g + 1, turn_b, samp_b)
        spread(g, samp_a)
        return carry

    lax.fori_loop(1, groups // 2, body, 0)
    spread(groups - 1, samp_b)
    for d in range(devices):
        out_ref[d] = ret[pl.ds(d * lines, lines), :].astype(jnp.bfloat16)


def bins(line, fetched, blocks, field, lines):
    count, samples, cells = blocks.shape
    devices = 2 * fetched.shape[0]
    group = 16
    return pl.pallas_call(
        functools.partial(bins_kernel, group),
        in_specs=[whole(), whole(), whole(pl.ANY), whole()],
        out_specs=[whole()] * 2,
        out_shape=[
            jax.ShapeDtypeStruct((devices, lines, LANES), jnp.bfloat16),
            jax.ShapeDtypeStruct(field.shape, jnp.float32),
        ],
        scratch_shapes=[pltpu.VMEM(blocks.shape, jnp.bfloat16)]
        + [pltpu.VMEM((group // 2, cells, 2 * samples), jnp.bfloat16)] * 2
        + [pltpu.VMEM((group // 2, SUB, 2 * samples), jnp.float32)] * 2
        + [pltpu.VMEM((devices * lines, LANES), jnp.float32)] * 2
        + [pltpu.SMEM(line.shape, jnp.int32), pltpu.SemaphoreType.DMA((count // group,)), pltpu.SemaphoreType.DMA],
        compiler_params=params(50),
        name="bins",
    )(line, fetched, blocks, field)


def image_kernel(near_vmem, far_vmem, arrived_ref, smooth_ref, direction_ref, residual_ref, image_ref, stats_ref, *scratch):
    *sums, near_ref, far_ref, sems = scratch
    copies = [
        pltpu.make_async_copy(a, b, sems.at[i]) for i, (a, b) in enumerate(((near_vmem, near_ref), (far_vmem, far_ref)))
    ]
    for copy in copies:
        copy.start()
    peers, cap = near_ref.shape[0], near_ref.shape[1] // 2
    beacons, rows, cols = direction_ref.shape
    bands, groups = rows // TILE_SIDE, cols // LANES
    span = lax.axis_size("tl")
    half = lax.axis_index("th")
    for total in sums:
        total[...] = jnp.zeros_like(total)
    for copy in copies:
        copy.wait()

    def body(q, carry):
        row, place = lax.div(q, span) * (2 * span), lax.rem(q, span)
        for away in range(2):
            d = row + (1 - half if away else half) * span + place
            for r in range(0, cap, 2):
                pair = arrived_ref[d, r * SUB : (r + 2) * SUB, :].astype(jnp.float32)
                for e in range(min(2, cap - r)):
                    first = far_ref[q, cap + r + e] - sums[0].shape[0] if away else near_ref[q, r + e]
                    if away:
                        first = jnp.maximum(first, 0)
                    at = pl.ds(pl.multiple_of(first, SUB), SUB)
                    sums[(r + e) % len(sums)][at, :] += pair[e * SUB : (e + 1) * SUB]
        return carry

    lax.fori_loop(0, peers, body, 0)
    lines = []
    units = []
    for k in range(beacons):
        unit = jnp.zeros((SUB, LANES), jnp.float32)
        for g in range(groups):
            x = []
            for band in range(bands):
                for h in range(2):
                    at = pl.ds((band * groups + g) * SUB * SUB + h * beacons + k, SUB, stride=SUB)
                    x.append(sum(total[at, :] for total in sums))
            x = jnp.concatenate(swap_chunks(x), axis=0)
            x = x + smooth_ref[k, :, g * LANES : (g + 1) * LANES]
            image_ref[k, :, g * LANES : (g + 1) * LANES] = x
            unit = jnp.maximum(unit, jnp.max(jnp.abs(x).reshape(bands * 2, SUB, LANES), axis=0))
        unit = jnp.maximum(unit, 1e-30)
        inverse = 1.0 / unit
        terms = [jnp.zeros((SUB, LANES), jnp.float32)] * 4
        for i in range(rows // SUB):
            for g in range(groups):
                at = (k, slice(i * SUB, (i + 1) * SUB), slice(g * LANES, (g + 1) * LANES))
                x, d, r = image_ref[at], direction_ref[at], residual_ref[at]
                scaled = x * inverse
                terms = [t + v for t, v in zip(terms, (r * r, d * x, r * scaled, scaled * scaled))]
        lines.append(terms)
        units.append(unit)
    largest = [jnp.max(unit, axis=(0, 1), keepdims=True) for unit in units]
    rows_of = []
    for q in range(4):
        for k in range(beacons):
            t = lines[k][q]
            if q >= 2:
                share = units[k] * (1.0 / largest[k])
                t = t * share if q == 2 else t * share * share
            rows_of.append(jnp.sum(t, axis=0, keepdims=True))
    for k in range(beacons):
        first = lax.broadcasted_iota(jnp.int32, (1, LANES), 1) == 0
        rows_of.append(jnp.where(first, largest[k], 0.0))
    rows_of.append(jnp.zeros((LANES - len(rows_of), LANES), jnp.float32))
    stats = jnp.sum(jnp.concatenate(rows_of, axis=0).T, axis=0, keepdims=True)
    stats_ref[...] = jnp.broadcast_to(stats, stats_ref.shape)


def image_of(near, far, arrived, smooth, direction, residual):
    beacons, rows, cols = direction.shape
    return pl.pallas_call(
        image_kernel,
        in_specs=[whole()] * 6,
        out_specs=[whole(), whole()],
        out_shape=[
            jax.ShapeDtypeStruct(direction.shape, jnp.float32),
            jax.ShapeDtypeStruct((arrived.shape[0], LANES), jnp.float32),
        ],
        scratch_shapes=[pltpu.VMEM((beacons * rows * cols // LANES, LANES), jnp.float32)] * 4
        + [pltpu.SMEM(near.shape, jnp.int32)] * 2
        + [pltpu.SemaphoreType.DMA((2,))],
        compiler_params=params(16),
        name="image",
    )(near, far, arrived, smooth, direction, residual)


def update_kernel(
    stats_ref, solution_ref, residual_ref, direction_ref, image_ref, sol_ref, res_ref, dir_ref, sol, res, dire, sems
):
    beacons = direction_ref.shape[0]
    stats = stats_ref[...]

    def column(x, q):
        return pltpu.roll(x, LANES - q * beacons, 1) if q else x

    total = jnp.sum(stats, axis=0, keepdims=True)
    total = jnp.broadcast_to(total, (SUB, LANES))
    alpha = total / column(total, 1)
    size = alpha[:1] * column(stats, 4)
    moved = jnp.sum(size * (size * column(stats, 3) - 2.0 * column(stats, 2)), axis=0, keepdims=True)
    beta = (total + moved) / total
    copies = []
    for k in range(beacons):
        a, b = alpha[:1, k : k + 1], beta[:1, k : k + 1]
        d = direction_ref[k]
        r = residual_ref[k] - a * image_ref[k]
        sol[k] = solution_ref[k] + a * d
        res[k] = r
        dire[k] = r + b * d
        for q, (held, out) in enumerate(((sol, sol_ref), (res, res_ref), (dire, dir_ref))):
            copies.append(pltpu.make_async_copy(held.at[k], out.at[k], sems.at[q, k]))
            copies[-1].start()
    for copy in copies:
        copy.wait()


def update(stats, solution, residual, direction, image):
    return pl.pallas_call(
        update_kernel,
        in_specs=[whole()] * 5,
        out_specs=[whole(pl.ANY)] * 3,
        out_shape=[jax.ShapeDtypeStruct(direction.shape, jnp.float32)] * 3,
        scratch_shapes=[pltpu.VMEM(direction.shape, jnp.float32)] * 3
        + [pltpu.SemaphoreType.DMA((3, direction.shape[0]))],
        compiler_params=params(16),
        name="update",
    )(stats, solution, residual, direction, image)


def exchange(x, axes):
    return lax.all_to_all(x, axes, split_axis=0, concat_axis=0, tiled=True)


def trade(x):
    return lax.ppermute(x, "th", [(0, 1), (1, 0)])


def per_device(solution, residual, direction, blocks, bin_owner, bin_tile):
    devices, span = lax.axis_size(AXES), lax.axis_size("tl")
    count = blocks.shape[0]
    cap = max(2, 3 * count // (2 * devices))
    lines = -(-cap // 2) * 2 * SUB
    beacons, rows, cols = direction.shape

    own, edges, direction = tiles(direction)
    other = trade(own)
    both = jnp.concatenate([bin_owner.reshape(1, count), bin_tile.reshape(1, count)], axis=0)
    line, request = prep(both, devices, cap, lines, span, rows * cols // TILE_SIDE**2)
    near = exchange(request.reshape(devices // 2, 2 * cap), HALF)
    far = trade(near)
    fetched = exchange(gather(near, own, other, edges, far, lines), HALF)
    returned, smoothed = bins(line, fetched, blocks, direction, lines)
    arrived = exchange(returned, AXES)
    image, stats = image_of(near, far, arrived, smoothed, direction, residual)
    return update(exchange(stats, AXES), solution, residual, direction, image)


def solution(mesh):
    rows, cols = mesh.devices.shape
    halves = jax.sharding.Mesh(mesh.devices.reshape(rows, 2, cols // 2), AXES)
    field = P(None, "tx", TY)
    return jax.shard_map(
        per_device,
        mesh=halves,
        in_specs=(field, field, field, P(AXES, None, None), P(AXES, None), P(AXES)),
        out_specs=(field,) * 3,
        check_vma=False,
    )
```

```python
import functools

import jax
import jax.numpy as jnp
from jax import lax
from jax.experimental import pallas as pl
from jax.experimental.pallas import tpu as pltpu
from jax.sharding import PartitionSpec as P

TILE_SIDE = 16
LANES = 128
SUB = 8
smooth_weight = 0.25

TY = ("th", "tl")
AXES = ("tx", "th", "tl")
HALF = ("tx", "tl")


def whole(memory=pltpu.VMEM):
    return pl.BlockSpec(memory_space=memory)


def params(mib):
    return pltpu.CompilerParams(vmem_limit_bytes=mib << 20)


def swap_chunks(blocks):
    row = lax.broadcasted_iota(jnp.int32, (SUB, LANES), 0)
    lane = lax.broadcasted_iota(jnp.int32, (SUB, LANES), 1)
    chunk, rest = lane // TILE_SIDE, lane % TILE_SIDE
    first = (chunk + row) % SUB * TILE_SIDE + rest
    second = (row - chunk + SUB) % SUB * TILE_SIDE + rest

    def swap(x):
        x = jnp.take_along_axis(x, first, axis=1)
        for s in (1, 2, 4):
            x = jnp.where((chunk & s) != 0, pltpu.roll(x, s, 0), x)
        return jnp.take_along_axis(x, second, axis=1)

    return [swap(x) for x in blocks]


def prep_kernel(step, span, tiles, both_ref, line_ref, request_ref):
    devices, bins = request_ref.shape[0], both_ref.shape[1]
    owner, tile = both_ref[:1], both_ref[1:]
    column = lax.rem(owner, 2 * span)
    far = (lax.div(column, span) != lax.axis_index("th")).astype(jnp.int32)
    place = (lax.div(owner, 2 * span) * span + lax.rem(column, span)) * 2 + far
    earlier = (
        lax.broadcasted_iota(jnp.int32, (bins, bins), 0) < lax.broadcasted_iota(jnp.int32, (bins, bins), 1)
    ).astype(jnp.bfloat16)
    member = (lax.broadcasted_iota(jnp.int32, (devices, bins), 0) == place).astype(jnp.float32)
    member16 = member.astype(jnp.bfloat16)
    before = jnp.dot(member16, earlier, preferred_element_type=jnp.float32)
    rank = jnp.sum(before * member, axis=0, keepdims=True).astype(jnp.int32)
    line_ref[:1] = place * step + rank * SUB
    line_ref[1:] = owner * step + rank * SUB
    at = lax.broadcasted_iota(jnp.int32, (request_ref.shape[1], bins), 0) == rank
    named = jnp.where(at, tile + far * tiles, 0).astype(jnp.float32).astype(jnp.bfloat16)
    request = lax.dot_general(member16, named, (((1,), (1,)), ((), ())), preferred_element_type=jnp.float32)
    request_ref[...] = request.astype(jnp.int32) * SUB


def prep(both, devices, cap, lines, span, tiles):
    bins = both.shape[1]
    return pl.pallas_call(
        functools.partial(prep_kernel, lines, span, tiles),
        in_specs=[whole()],
        out_specs=[whole()] * 2,
        out_shape=[
            jax.ShapeDtypeStruct((2, bins), jnp.int32),
            jax.ShapeDtypeStruct((devices, cap), jnp.int32),
        ],
        compiler_params=params(4),
        name="prep",
    )(both)


def tiles_kernel(field_ref, out_ref, edges_ref, copy_ref, held):
    beacons, rows, cols = field_ref.shape
    bands, groups = rows // TILE_SIDE, cols // LANES
    for k in range(beacons):
        for g in range(groups):
            x = field_ref[k, :, g * LANES : (g + 1) * LANES]
            x = swap_chunks([x[i * SUB : (i + 1) * SUB] for i in range(bands * 2)])
            for band in range(bands):
                for h in range(2):
                    at = (band * groups + g) * SUB * SUB + h * beacons + k
                    held[pl.ds(at, SUB, stride=SUB), :] = x[band * 2 + h]
    copy_ref[...] = field_ref[...]
    count = held.shape[0]
    out_ref[:count] = held[...].astype(jnp.bfloat16)
    ends = [field_ref[k, r : r + 1, g * LANES : (g + 1) * LANES] for r in (0, rows - 1) for k in range(beacons) for g in range(groups)]
    edges_ref[...] = jnp.concatenate(ends, axis=0).astype(jnp.bfloat16)
    lane = lax.broadcasted_iota(jnp.int32, (rows, LANES), 1)
    sides = jnp.zeros((rows, LANES), jnp.float32)
    for k in range(beacons):
        sides = jnp.where(lane == k, field_ref[k, :, cols - 1 :], sides)
        sides = jnp.where(lane == beacons + k, field_ref[k, :, :1], sides)
    out_ref[count:] = sides.T[: 2 * SUB].astype(jnp.bfloat16)


def tiles(field):
    beacons, rows, cols = field.shape
    return pl.pallas_call(
        tiles_kernel,
        in_specs=[whole()],
        out_specs=[whole()] * 3,
        out_shape=[
            jax.ShapeDtypeStruct((beacons * rows * cols // LANES + 2 * SUB, LANES), jnp.bfloat16),
            jax.ShapeDtypeStruct((2 * SUB, LANES), jnp.bfloat16),
            jax.ShapeDtypeStruct(field.shape, field.dtype),
        ],
        scratch_shapes=[pltpu.VMEM((beacons * rows * cols // LANES, LANES), jnp.float32)],
        compiler_params=params(8),
        name="tiles",
    )(field)


def gather_kernel(cap, wanted_vmem, own_ref, other_ref, edges_ref, after_ref, out_ref, held, wanted_ref, sem):
    copy = pltpu.make_async_copy(wanted_vmem, wanted_ref, sem)
    copy.start()
    peers, lines = wanted_ref.shape[0], out_ref.shape[1] // 2 - SUB
    rows = held.shape[0] // 2
    held[:rows] = own_ref[:rows].astype(jnp.float32)
    held[rows:] = other_ref[:rows].astype(jnp.float32)
    copy.wait()

    def at(d, r):
        return held[pl.ds(pl.multiple_of(wanted_ref[d, r], SUB), SUB), :]

    def body(d, carry):
        for block in range(2):
            for r in range(0, cap, 2):
                to = block * lines + r * SUB
                one = at(d, block * cap + r)
                two = at(d, block * cap + r + 1) if r + 1 < cap else jnp.zeros_like(one)
                out_ref[d, to : to + 2 * SUB, :] = jnp.concatenate([one, two], axis=0).astype(jnp.bfloat16)
        return carry

    lax.fori_loop(0, peers, body, 0, unroll=2)

    tx, th, tl = (lax.axis_index(axis) for axis in AXES)
    deep, span = lax.axis_size("tx"), lax.axis_size("tl")
    edges = edges_ref[...].astype(jnp.float32)
    none = jnp.zeros((SUB, LANES), jnp.float32)
    own = jnp.concatenate([none, own_ref[rows:].astype(jnp.float32)[:SUB]], axis=0).astype(jnp.bfloat16)
    other = jnp.concatenate([none, other_ref[rows:].astype(jnp.float32)[:SUB]], axis=0).astype(jnp.bfloat16)
    top = jnp.concatenate([edges[:SUB], none], axis=0).astype(jnp.bfloat16)
    bottom = jnp.concatenate([edges[SUB:], none], axis=0).astype(jnp.bfloat16)
    for there, x, y, block in (
        (tx > 0, tx - 1, tl, top),
        (tx < deep - 1, tx + 1, tl, bottom),
        (tl > 0, tx, tl - 1, own),
        (tl < span - 1, tx, tl + 1, own),
        ((th == 0) & (tl == 0), tx, span - 1, other),
        ((th == 1) & (tl == span - 1), tx, 0, other),
    ):

        @pl.when(there)
        def _(x=x, y=y, block=block):
            out_ref[jnp.clip(x * span + y, 0, peers - 1), 2 * lines :, :] = block


def gather(wanted, own, other, edges, after, lines):
    peers = wanted.shape[0]
    return pl.pallas_call(
        functools.partial(gather_kernel, wanted.shape[1] // 2),
        in_specs=[whole()] * 4 + [whole(pl.ANY)],
        out_specs=whole(),
        out_shape=jax.ShapeDtypeStruct((peers, 2 * lines + 2 * SUB, LANES), jnp.bfloat16),
        scratch_shapes=[
            pltpu.VMEM((2 * own.shape[0] - 4 * SUB, LANES), jnp.float32),
            pltpu.SMEM(wanted.shape, jnp.int32),
            pltpu.SemaphoreType.DMA,
        ],
        compiler_params=params(8),
        name="gather",
    )(wanted, own, other, edges, after)


def smooth(field_ref, fetched_ref, at, out_ref):
    beacons, rows, cols = field_ref.shape
    tx, th, tl = (lax.axis_index(axis) for axis in AXES)
    deep, span = lax.axis_size("tx"), lax.axis_size("tl")
    peers = fetched_ref.shape[0]

    def edge(there, x, y):
        peer = jnp.clip(x * span + y, 0, peers - 1)
        return jnp.where(there, fetched_ref[peer, at : at + 2 * SUB, :].astype(jnp.float32), 0.0)

    def line_of(block, k):
        return jnp.concatenate([block[2 * k : 2 * k + 1], block[2 * k + 1 : 2 * k + 2]], axis=1)

    above, below = edge(tx > 0, tx - 1, tl), edge(tx < deep - 1, tx + 1, tl)
    left = edge((tl > 0) | (th == 1), tx, jnp.where(tl > 0, tl - 1, span - 1))
    right = edge((tl < span - 1) | (th == 0), tx, jnp.where(tl < span - 1, tl + 1, 0))
    sides = jnp.concatenate([left[SUB : SUB + beacons], right[SUB + beacons : SUB + 2 * beacons]], axis=0).T
    row = lax.broadcasted_iota(jnp.int32, (rows, cols), 0)
    col = lax.broadcasted_iota(jnp.int32, (rows, cols), 1)
    for k in range(beacons):
        x = field_ref[k]
        near = jnp.where(row == 0, line_of(above, k), pltpu.roll(x, 1, 0))
        near += jnp.where(row == rows - 1, line_of(below, k), pltpu.roll(x, rows - 1, 0))
        near += jnp.where(col == 0, sides[:, k : k + 1], pltpu.roll(x, 1, 1))
        near += jnp.where(col == cols - 1, sides[:, beacons + k : beacons + k + 1], pltpu.roll(x, cols - 1, 1))
        out_ref[k] = smooth_weight * (4.0 * x - near)


def bins_kernel(
    group, line_vmem, fetched_ref, blocks_ref, field_ref, out_ref, smooth_ref, *scratch
):
    held_ref, turn_a, turn_b, samp_a, samp_b, pick, ret, line_ref, sems, sem = scratch
    devices, lines, _ = out_ref.shape
    count, samples, cells = blocks_ref.shape
    groups, pairs = count // group, group // 2

    def fetch(i):
        part = pl.ds(i * group, group)
        return pltpu.make_async_copy(blocks_ref.at[part], held_ref.at[part], sems.at[i])

    for i in range(groups):
        fetch(i).start()
    copy = pltpu.make_async_copy(line_vmem, line_ref, sem)
    copy.start()
    for d in range(devices):
        pick[pl.ds(d * lines, lines), :] = fetched_ref[d // 2, d % 2 * lines : (d % 2 + 1) * lines, :].astype(jnp.float32)
        ret[pl.ds(d * lines, lines), :] = jnp.zeros((lines, LANES), jnp.float32)
    smooth(field_ref, fetched_ref, 2 * lines, smooth_ref)
    low = lax.broadcasted_iota(jnp.int32, (SUB, LANES), 0) < 4

    def weights(g, p):
        return held_ref[pl.ds(g * group + 2 * p, 2)].reshape(2 * samples, cells)

    def turn(g, to):
        for p in range(pairs):
            to[p] = weights(g, p).T

    def line(b, back):
        return pl.ds(pl.multiple_of(line_ref[back, b], SUB), SUB)

    def sample(g, turned, to):
        for p in range(pairs):
            f0 = pick[line(g * group + 2 * p, 0), :]
            f1 = pick[line(g * group + 2 * p + 1, 0), :]
            left = jnp.where(low, f0, pltpu.roll(f1, 4, 0))
            right = jnp.where(low, pltpu.roll(f0, 4, 0), f1)
            x = jnp.concatenate([left, right], axis=1).astype(jnp.bfloat16)
            s = jnp.dot(x, turned[p], preferred_element_type=jnp.float32)
            to[p] = jnp.concatenate([jnp.where(low, s[:, :samples], 0.0), jnp.where(low, 0.0, s[:, samples:])], axis=1)

    def spread(g, sampled):
        for p in range(pairs):
            a = jnp.dot(sampled[p].astype(jnp.bfloat16), weights(g, p), preferred_element_type=jnp.float32)
            left, right = a[:, :LANES], a[:, LANES:]
            ret[line(g * group + 2 * p, 1), :] = jnp.where(low, left, pltpu.roll(right, 4, 0))
            ret[line(g * group + 2 * p + 1, 1), :] = jnp.where(low, pltpu.roll(left, 4, 0), right)

    copy.wait()
    fetch(0).wait()
    turn(0, turn_a)
    fetch(1).wait()
    turn(1, turn_b)
    sample(0, turn_a, samp_a)
    fetch(2).wait()
    turn(2, turn_a)
    sample(1, turn_b, samp_b)
    spread(0, samp_a)

    def body(i, carry):
        g = 2 * i
        fetch(g + 1).wait()

        @pl.when(g + 2 < groups)
        def _():
            fetch(g + 2).wait()

        turn(g + 1, turn_b)
        sample(g, turn_a, samp_a)
        spread(g - 1, samp_b)
        turn(jnp.minimum(g + 2, groups - 1), turn_a)
        sample(g + 1, turn_b, samp_b)
        spread(g, samp_a)
        return carry

    lax.fori_loop(1, groups // 2, body, 0)
    spread(groups - 1, samp_b)
    for d in range(devices):
        out_ref[d] = ret[pl.ds(d * lines, lines), :].astype(jnp.bfloat16)


def bins(line, fetched, blocks, field, lines):
    count, samples, cells = blocks.shape
    devices = 2 * fetched.shape[0]
    group = 16
    return pl.pallas_call(
        functools.partial(bins_kernel, group),
        in_specs=[whole(), whole(), whole(pl.ANY), whole()],
        out_specs=[whole()] * 2,
        out_shape=[
            jax.ShapeDtypeStruct((devices, lines, LANES), jnp.bfloat16),
            jax.ShapeDtypeStruct(field.shape, jnp.float32),
        ],
        scratch_shapes=[pltpu.VMEM(blocks.shape, jnp.bfloat16)]
        + [pltpu.VMEM((group // 2, cells, 2 * samples), jnp.bfloat16)] * 2
        + [pltpu.VMEM((group // 2, SUB, 2 * samples), jnp.float32)] * 2
        + [pltpu.VMEM((devices * lines, LANES), jnp.float32)] * 2
        + [pltpu.SMEM(line.shape, jnp.int32), pltpu.SemaphoreType.DMA((count // group,)), pltpu.SemaphoreType.DMA],
        compiler_params=params(50),
        name="bins",
    )(line, fetched, blocks, field)


def image_kernel(near_vmem, far_vmem, arrived_ref, smooth_ref, direction_ref, residual_ref, image_ref, stats_ref, *scratch):
    *sums, near_ref, far_ref, sems = scratch
    copies = [
        pltpu.make_async_copy(a, b, sems.at[i]) for i, (a, b) in enumerate(((near_vmem, near_ref), (far_vmem, far_ref)))
    ]
    for copy in copies:
        copy.start()
    peers, cap = near_ref.shape[0], near_ref.shape[1] // 2
    beacons, rows, cols = direction_ref.shape
    bands, groups = rows // TILE_SIDE, cols // LANES
    span = lax.axis_size("tl")
    half = lax.axis_index("th")
    for total in sums:
        total[...] = jnp.zeros_like(total)
    for copy in copies:
        copy.wait()

    def body(q, carry):
        row, place = lax.div(q, span) * (2 * span), lax.rem(q, span)
        for away in range(2):
            d = row + (1 - half if away else half) * span + place
            for r in range(0, cap, 2):
                pair = arrived_ref[d, r * SUB : (r + 2) * SUB, :].astype(jnp.float32)
                for e in range(min(2, cap - r)):
                    first = far_ref[q, cap + r + e] - sums[0].shape[0] if away else near_ref[q, r + e]
                    if away:
                        first = jnp.maximum(first, 0)
                    at = pl.ds(pl.multiple_of(first, SUB), SUB)
                    sums[(r + e) % len(sums)][at, :] += pair[e * SUB : (e + 1) * SUB]
        return carry

    lax.fori_loop(0, peers, body, 0)
    lines = []
    units = []
    for k in range(beacons):
        unit = jnp.zeros((SUB, LANES), jnp.float32)
        for g in range(groups):
            x = []
            for band in range(bands):
                for h in range(2):
                    at = pl.ds((band * groups + g) * SUB * SUB + h * beacons + k, SUB, stride=SUB)
                    x.append(sum(total[at, :] for total in sums))
            x = jnp.concatenate(swap_chunks(x), axis=0)
            x = x + smooth_ref[k, :, g * LANES : (g + 1) * LANES]
            image_ref[k, :, g * LANES : (g + 1) * LANES] = x
            unit = jnp.maximum(unit, jnp.max(jnp.abs(x).reshape(bands * 2, SUB, LANES), axis=0))
        unit = jnp.maximum(unit, 1e-30)
        inverse = 1.0 / unit
        terms = [jnp.zeros((SUB, LANES), jnp.float32)] * 4
        for i in range(rows // SUB):
            for g in range(groups):
                at = (k, slice(i * SUB, (i + 1) * SUB), slice(g * LANES, (g + 1) * LANES))
                x, d, r = image_ref[at], direction_ref[at], residual_ref[at]
                scaled = x * inverse
                terms = [t + v for t, v in zip(terms, (r * r, d * x, r * scaled, scaled * scaled))]
        lines.append(terms)
        units.append(unit)
    largest = [jnp.max(unit, axis=(0, 1), keepdims=True) for unit in units]
    rows_of = []
    for q in range(4):
        for k in range(beacons):
            t = lines[k][q]
            if q >= 2:
                share = units[k] * (1.0 / largest[k])
                t = t * share if q == 2 else t * share * share
            rows_of.append(jnp.sum(t, axis=0, keepdims=True))
    for k in range(beacons):
        first = lax.broadcasted_iota(jnp.int32, (1, LANES), 1) == 0
        rows_of.append(jnp.where(first, largest[k], 0.0))
    rows_of.append(jnp.zeros((LANES - len(rows_of), LANES), jnp.float32))
    stats = jnp.sum(jnp.concatenate(rows_of, axis=0).T, axis=0, keepdims=True)
    stats_ref[...] = jnp.broadcast_to(stats, stats_ref.shape)


def image_of(near, far, arrived, smooth, direction, residual):
    beacons, rows, cols = direction.shape
    return pl.pallas_call(
        image_kernel,
        in_specs=[whole()] * 6,
        out_specs=[whole(), whole()],
        out_shape=[
            jax.ShapeDtypeStruct(direction.shape, jnp.float32),
            jax.ShapeDtypeStruct((arrived.shape[0], LANES), jnp.float32),
        ],
        scratch_shapes=[pltpu.VMEM((beacons * rows * cols // LANES, LANES), jnp.float32)] * 4
        + [pltpu.SMEM(near.shape, jnp.int32)] * 2
        + [pltpu.SemaphoreType.DMA((2,))],
        compiler_params=params(16),
        name="image",
    )(near, far, arrived, smooth, direction, residual)


def update_kernel(
    stats_ref, solution_ref, residual_ref, direction_ref, image_ref, sol_ref, res_ref, dir_ref, sol, res, dire, sems
):
    beacons = direction_ref.shape[0]
    stats = stats_ref[...]

    def column(x, q):
        return pltpu.roll(x, LANES - q * beacons, 1) if q else x

    total = jnp.sum(stats, axis=0, keepdims=True)
    total = jnp.broadcast_to(total, (SUB, LANES))
    alpha = total / column(total, 1)
    size = alpha[:1] * column(stats, 4)
    moved = jnp.sum(size * (size * column(stats, 3) - 2.0 * column(stats, 2)), axis=0, keepdims=True)
    beta = (total + moved) / total
    copies = []

    def send(q, k, held, out):
        copies.append(pltpu.make_async_copy(held.at[k], out.at[k], sems.at[q, k]))
        copies[-1].start()

    for k in range(beacons):
        sol[k] = solution_ref[k] + alpha[:1, k : k + 1] * direction_ref[k]
        send(0, k, sol, sol_ref)
    for k in range(beacons):
        res[k] = residual_ref[k] - alpha[:1, k : k + 1] * image_ref[k]
        send(1, k, res, res_ref)
    for k in range(beacons):
        dire[k] = res[k] + beta[:1, k : k + 1] * direction_ref[k]
        send(2, k, dire, dir_ref)
    for copy in copies:
        copy.wait()


def update(stats, solution, residual, direction, image):
    return pl.pallas_call(
        update_kernel,
        in_specs=[whole()] * 5,
        out_specs=[whole(pl.ANY)] * 3,
        out_shape=[jax.ShapeDtypeStruct(direction.shape, jnp.float32)] * 3,
        scratch_shapes=[pltpu.VMEM(direction.shape, jnp.float32)] * 3
        + [pltpu.SemaphoreType.DMA((3, direction.shape[0]))],
        compiler_params=params(16),
        name="update",
    )(stats, solution, residual, direction, image)


def exchange(x, axes):
    return lax.all_to_all(x, axes, split_axis=0, concat_axis=0, tiled=True)


def trade(x):
    return lax.ppermute(x, "th", [(0, 1), (1, 0)])


def per_device(solution, residual, direction, blocks, bin_owner, bin_tile):
    devices, span = lax.axis_size(AXES), lax.axis_size("tl")
    count = blocks.shape[0]
    cap = max(2, 3 * count // (2 * devices))
    lines = -(-cap // 2) * 2 * SUB
    beacons, rows, cols = direction.shape

    own, edges, direction = tiles(direction)
    other = trade(own)
    both = jnp.concatenate([bin_owner.reshape(1, count), bin_tile.reshape(1, count)], axis=0)
    line, request = prep(both, devices, cap, lines, span, rows * cols // TILE_SIDE**2)
    near = exchange(request.reshape(devices // 2, 2 * cap), HALF)
    far = trade(near)
    fetched = exchange(gather(near, own, other, edges, far, lines), HALF)
    returned, smoothed = bins(line, fetched, blocks, direction, lines)
    arrived = exchange(returned, AXES)
    image, stats = image_of(near, far, arrived, smoothed, direction, residual)
    return update(exchange(stats, AXES), solution, residual, direction, image)


def solution(mesh):
    rows, cols = mesh.devices.shape
    halves = jax.sharding.Mesh(mesh.devices.reshape(rows, 2, cols // 2), AXES)
    field = P(None, "tx", TY)
    return jax.shard_map(
        per_device,
        mesh=halves,
        in_specs=(field, field, field, P(AXES, None, None), P(AXES, None), P(AXES)),
        out_specs=(field,) * 3,
        check_vma=False,
    )
```
